256 devices in a mesh: comp: 4 (over z_lo, core), seq: 64 (over z_hi, y, x).
Axes of the slice: x: 4, y: 4, z: 8 (z_hi: 4, z_lo: 2; z = z_hi * 2 + z_lo), core: 2. Of those that a mesh axis runs over, the one named last changes fastest.
Arguments:
- latent_video: bfloat16 [2048, 1536], P('seq'), may hold values from -6 to 6
- text_embed: bfloat16 [256, 1536], P('seq'), may hold values from -6 to 6
- previous_video: bfloat16 [4, 2048, 1536], P('comp', 'seq'), may hold values from -6 to 6
- previous_text: bfloat16 [4, 256, 1536], P('comp', 'seq'), may hold values from -6 to 6
- noise_blend: float32 [50, 2], replicated, may hold values from 0.3 to 1.2
- modulation: float32 [4, 50, 2, 3, 1536], P('comp'), may hold values from -4 to 4
- w_qkv: bfloat16 [4, 2, 3, 1536, 1536], P('comp', None, None, None, 'seq'), may hold values from -0.15625 to 0.15625
- w_out: bfloat16 [4, 2, 1536, 1536], P('comp', None, None, 'seq'), may hold values from -0.15625 to 0.15625
- qk_gain: float32 [4, 2, 2, 128], P('comp'), may hold values from 1 to 10
- text_len: int32 [4], replicated, may hold values from 1 to 256
- timestep: int32 [1], replicated, may hold values from 0 to 49
Outputs:
- video_out: bfloat16 [4, 2048, 1536], P('comp', 'seq')
- text_out: bfloat16 [4, 256, 1536], P('comp', 'seq')
The draws below stay inside these ranges and needn't reach their ends.
All inputs are finite; a program needn't handle non-finite values.
Results may differ from the reference program's by a relative error of at most 0.04.
Values may be sent and summed in bfloat16 or wider, within the bound.
A program may use at most 128 MiB of HBM per device.

```python
import math
import jax
import jax.numpy as jnp
from jax import lax

D = 1536
HEADS = 12
HEAD_DIM = 128
INNER = 1536
STEPS = 50
COMP = 4
NV = 2048
TXT = 256


def draw_qk_gain(key, part):
    key = jax.random.fold_in(key, 7)
    lower = math.log(1.0)
    upper = math.log(2.5)
    exponent = jax.random.uniform(key, (COMP, 2, 2, HEAD_DIM), jnp.float32, lower, upper)
    return jnp.exp(exponent).astype(jnp.float32)


def place_ends(result, own_key, least, top_value):
    shape = result.shape
    place = [jax.random.randint(jax.random.fold_in(own_key, axis), (), 0, shape[axis]) for axis in range(len(shape))]
    result = result.at[tuple(place)].set(least)
    longest = shape.index(max(shape))
    place[longest] = (place[longest] + 1) % shape[longest]
    return result.at[tuple(place)].set(top_value)


def block_levels(stream_key, extent, split, smallest, high):
    loudness, own = 1.0, jax.random.fold_in(stream_key, 6)
    for dim, parts in split:
        steps = jnp.exp(jax.random.uniform(jax.random.fold_in(own, dim), (parts,), jnp.float32, smallest / len(split), high / len(split)))
        loudness = loudness * jnp.repeat(steps, extent[dim] // parts).reshape([-1 if axis == dim else 1 for axis in range(len(extent))])
    return loudness


def scatter_about(key, shape, width, bound, cuts=(), held_as=jnp.bfloat16):
    factor_of = block_levels(key, shape, cuts, -0.22, 0.18) if cuts else 1.0
    array = jax.random.normal(key, shape, jnp.float32) * width * factor_of
    return jnp.minimum(jnp.maximum(array, -bound), bound).astype(held_as)


def setup_inputs(seed: int = 0) -> dict:
    splits = jax.random.split(jax.random.key(seed), 12)
    latent_video = scatter_about(splits[0], (NV, D), 1.0, 6.0, ((0, 64),))
    text_embed = scatter_about(splits[1], (TXT, D), 1.0, 6.0, ((0, 64),))
    previous_video = scatter_about(splits[2], (COMP, NV, D), 1.0, 6.0, ((0, 4), (1, 64)))
    previous_text = scatter_about(splits[3], (COMP, TXT, D), 1.0, 6.0, ((0, 4), (1, 64)))
    noise_blend = jnp.clip(jax.random.uniform(splits[4], (STEPS, 2), jnp.float32, 0.3, 1.2), 0.3, 1.2)
    modulation = scatter_about(splits[5], (COMP, STEPS, 2, 3, D), 1.0, 4.0, ((0, 4),), jnp.float32)
    w_qkv = scatter_about(splits[6], (COMP, 2, 3, D, INNER), D ** -0.5, 0.15625, ((0, 4), (4, 64)))
    w_out = scatter_about(splits[7], (COMP, 2, INNER, D), INNER ** -0.5, 0.15625, ((0, 4), (3, 64)))
    qk_gain = draw_qk_gain(jax.random.fold_in(splits[11], 71), 0)
    text_len = place_ends(jax.random.randint(splits[9], (COMP,), 1, TXT + 1), jax.random.fold_in(splits[9], 1), 1, TXT).astype(jnp.int32)
    timestep = jax.random.randint(splits[10], (1,), 0, STEPS).astype(jnp.int32)
    return {"latent_video": latent_video, "text_embed": text_embed, "previous_video": previous_video, "previous_text": previous_text, "noise_blend": noise_blend, "modulation": modulation, "w_qkv": w_qkv, "w_out": w_out, "qk_gain": qk_gain, "text_len": text_len, "timestep": timestep}


def layer_norm(values, shift, scale):
    wide = values.astype(jnp.float32)
    center = wide - lax.optimization_barrier(jnp.mean(wide, axis=-1, keepdims=True))
    spread = lax.optimization_barrier(jnp.mean(center * center, axis=-1, keepdims=True))
    return (center * lax.rsqrt(spread + 1e-06) * (1.0 + scale) + shift).astype(jnp.bfloat16)

def head_norm(values, gain):
    wide = values.astype(jnp.float32).reshape(values.shape[:-1] + (HEADS, HEAD_DIM))
    square = lax.optimization_barrier(jnp.mean(wide * wide, axis=-1, keepdims=True))
    return (wide * lax.rsqrt(square + 1e-06) * gain).reshape(values.shape).astype(jnp.bfloat16)

def to_heads(tensor):
    return tensor.reshape(tensor.shape[0], HEADS, HEAD_DIM).transpose(1, 0, 2)

def attend(queries, key_rows, value_rows, usable):
    row_total = queries.shape[0]
    factor = 1.0 / math.sqrt(HEAD_DIM)

    def one_head(operands):
        query_head, key_head, value_head = operands
        scores = jnp.dot(query_head, key_head.T, preferred_element_type=jnp.float32) * factor
        scores = jnp.where(usable[None, :], scores, -1e+30)
        highest = lax.optimization_barrier(jnp.max(scores, axis=-1, keepdims=True))
        weights = jnp.where(usable[None, :], jnp.exp(scores - highest), 0.0)
        totals = lax.optimization_barrier(jnp.sum(weights, axis=-1, keepdims=True))
        mixed = jnp.dot(weights.astype(jnp.bfloat16), value_head, preferred_element_type=jnp.float32)
        return mixed / totals
    heads_out = lax.map(one_head, (to_heads(queries), to_heads(key_rows), to_heads(value_rows)))
    return heads_out.transpose(1, 0, 2).reshape(row_total, HEADS * HEAD_DIM).astype(jnp.bfloat16)

def reference(latent_video, text_embed, previous_video, previous_text, noise_blend, modulation, w_qkv, w_out, qk_gain, text_len, timestep):
    step_index = timestep[0]
    blend_row = noise_blend[step_index]
    video_count = latent_video.shape[0]
    video_list = []
    text_list = []
    for component in range(COMP):
        usable = jnp.concatenate([jnp.ones((video_count,), bool), jnp.arange(text_embed.shape[0], dtype=jnp.int32) < text_len[component]])
        if component == 0:
            video_in = (blend_row[0] * latent_video.astype(jnp.float32) + blend_row[1] * previous_video[COMP - 1].astype(jnp.float32)).astype(jnp.bfloat16)
            text_in = text_embed
        else:
            video_in = previous_video[component - 1]
            text_in = previous_text[component - 1]
        modulate = modulation[component, step_index]
        normed_video = layer_norm(video_in, modulate[0, 0], modulate[0, 1])
        normed_text = layer_norm(text_in, modulate[1, 0], modulate[1, 1])
        proj_video = [jnp.dot(normed_video, w_qkv[component, 0, which], preferred_element_type=jnp.float32).astype(jnp.bfloat16) for which in range(3)]
        proj_text = [jnp.dot(normed_text, w_qkv[component, 1, which], preferred_element_type=jnp.float32).astype(jnp.bfloat16) for which in range(3)]
        queries = jnp.concatenate([head_norm(proj_video[0], qk_gain[component, 0, 0]), head_norm(proj_text[0], qk_gain[component, 1, 0])])
        key_rows = jnp.concatenate([head_norm(proj_video[1], qk_gain[component, 0, 1]), head_norm(proj_text[1], qk_gain[component, 1, 1])])
        value_rows = jnp.concatenate([proj_video[2], proj_text[2]])
        attended = attend(queries, key_rows, value_rows, usable)
        projected_video = jnp.dot(attended[:video_count], w_out[component, 0], preferred_element_type=jnp.float32).astype(jnp.bfloat16)
        projected_text = jnp.dot(attended[video_count:], w_out[component, 1], preferred_element_type=jnp.float32).astype(jnp.bfloat16)
        video_list.append((video_in.astype(jnp.float32) + modulate[0, 2] * projected_video.astype(jnp.float32)).astype(jnp.bfloat16))
        text_list.append((text_in.astype(jnp.float32) + modulate[1, 2] * projected_text.astype(jnp.float32)).astype(jnp.bfloat16))
    return (jnp.stack(video_list), jnp.stack(text_list))
```

```python
import math

import jax
import jax.numpy as jnp
from jax import lax
from jax.experimental import pallas as pl
from jax.experimental.pallas import tpu as pltpu
from jax.sharding import PartitionSpec as P

HEAD_DIM = 128
F32, BF16 = jnp.float32, jnp.bfloat16
MESH = pl.DeviceIdType.MESH
FACTOR = 1.0 / math.sqrt(HEAD_DIM)


def kernel(
    latent, text, prev_v, prev_t, blend, mod, gains, text_len, wqkv, wout,
    vout, tout,
    vsend, pack32, tsend, zv, zt, tokv, tokt, wq,
    b, kv, qraw, qtraw, qall, kn, vall,
    osend, ssend, orecv, srecv, otrecv, strecv,
    woz, wov, wot, pout, precv, tpart, tpack, trecv, ttout,
    send, r_z, r_w, r_y, r_q, r_qt, r_kv, r_qx, r_o, r_ot,
    r_woz, r_wox, r_woy, r_woyt, r_out, r_tp, loc,
):
    c = lax.axis_index("comp")
    s = lax.axis_index("seq")
    z, y, x = s // 16, (s // 4) % 4, s % 4
    diag = y == x

    def at_seq(comp, zz, yy, xx):
        return (comp, zz * 16 + yy * 4 + xx)

    def zpeer(d):
        return at_seq(c, (z + d) % 4, y, x)

    def ypeer(d):
        return at_seq(c, z, (y + d) % 4, x)

    def xpeer(d):
        return at_seq(c, z, y, (x + d) % 4)

    used = [0]
    always, on_diag, off_diag = [], [], []

    def copy_to(src, dst, recv, device, group=None):
        op = pltpu.make_async_remote_copy(
            src_ref=src, dst_ref=dst, send_sem=send.at[used[0]], recv_sem=recv,
            device_id=device, device_id_type=MESH,
        )
        used[0] += 1
        op.start()
        (always if group is None else group).append(op)

    def arrived(dst, recv):
        pltpu.make_async_remote_copy(
            src_ref=dst, dst_ref=dst, send_sem=send.at[0], recv_sem=recv,
            device_id=xpeer(1), device_id_type=MESH,
        ).wait_recv()

    nextc, prevc = (c + 1) % 4, (c + 3) % 4
    barrier = pltpu.get_barrier_semaphore()
    for d in range(4):
        pl.semaphore_signal(barrier, inc=1, device_id=at_seq(prevc, (z + d) % 4, y, x), device_id_type=MESH)
    for d in (1, 2, 3):
        for peer in (zpeer, ypeer, xpeer):
            pl.semaphore_signal(barrier, inc=1, device_id=peer(d), device_id_type=MESH)

    own_w = pltpu.make_async_copy(wqkv, wq.at[x], loc.at[0])
    own_w.start()
    own_o = pltpu.make_async_copy(wout, woz.at[0], loc.at[1])
    own_o.start()

    last = c == 3
    old = prev_v[...]
    mixed = (blend[0] * latent[...].astype(F32) + blend[1] * old.astype(F32)).astype(BF16)
    vsend[...] = jnp.where(last, mixed, old)
    words = jnp.where(last, text[...], prev_t[...]).astype(F32)
    for j in range(4):
        pack32[4 * j : 4 * j + 4, :] = words[:, 384 * j : 384 * j + 384]
    tsend[...] = pack32[...].astype(BF16)
    tokt[4:8] = jnp.zeros((4, 16, 1536), BF16)

    pl.semaphore_wait(barrier, 13)

    for d in (0, 1, 3, 2):
        copy_to(vsend, zv.at[z], r_z.at[d, 0], at_seq(nextc, (z + d) % 4, y, x))
        copy_to(tsend, zt.at[z], r_z.at[d, 1], at_seq(nextc, (z + d) % 4, y, x))
    for d in (1, 3, 2):
        copy_to(wqkv, wq.at[x], r_w.at[d - 1], xpeer(d))
    own_o.wait()
    for d in (1, 3, 2):
        there = pl.multiple_of(((z + d) % 4) * 384, 128)
        copy_to(woz.at[0, :, pl.ds(there, 384)], woz.at[d, :, 0:384], r_woz.at[d - 1], zpeer(d))

    def normed(wide, stream):
        center = wide - jnp.mean(wide, axis=-1, keepdims=True)
        spread = jnp.mean(center * center, axis=-1, keepdims=True)
        shift = mod[3 * stream : 3 * stream + 1, :]
        scale = mod[3 * stream + 1 : 3 * stream + 2, :]
        return (center * lax.rsqrt(spread + 1e-06) * (1.0 + scale) + shift).astype(BF16)

    def unpack(packed):
        return jnp.concatenate([packed[4 * j : 4 * j + 4, :] for j in range(4)], axis=1)

    for d in (0, 1, 3, 2):
        zz = (z + 4 - d) % 4
        arrived(zv.at[zz], r_z.at[d, 0])
        slot = y * 4 + zz
        tokv[slot] = normed(zv[zz].astype(F32), 0)
        for e in (1, 3, 2):
            copy_to(tokv.at[slot], tokv.at[slot], r_y.at[e - 1, d], ypeer(e))
    for d in (0, 1, 3, 2):
        arrived(zt.at[(z + 4 - d) % 4], r_z.at[d, 1])
    rows = jnp.concatenate([unpack(zt[j].astype(F32)) for j in range(4)], axis=0)
    tokt[y] = normed(rows, 1)
    for e in (1, 3, 2):
        copy_to(tokt.at[y], tokt.at[y], r_y.at[e - 1, 4], ypeer(e))

    own_w.wait()
    for d in (1, 3, 2):
        arrived(wq.at[(x + 4 - d) % 4], r_w.at[d - 1])
    weights = wq[...].reshape(576, 1536)

    def project(tokens, stream):
        out = lax.dot_general(
            weights, tokens, (((1,), (1,)), ((), ())), preferred_element_type=F32
        )
        return jnp.concatenate(
            [
                out[xx * 144 + stream * 72 + j * 24 :][:24]
                for j in range(3)
                for xx in range(4)
            ],
            axis=0,
        ).astype(BF16)

    for k, d in enumerate((0, 1, 3, 2)):
        yy = (y + 4 - d) % 4
        if d:
            for dz in range(4):
                arrived(tokv.at[yy * 4 + dz], r_y.at[d - 1, dz])
        b[k] = project(tokv[pl.ds(yy * 4, 4)].reshape(128, 1536), 0)
        if d:
            copy_to(b.at[k, 0:96], qraw.at[y], r_q.at[d - 1], ypeer(4 - d))
        else:
            qraw[y] = b[k, 0:96]
        for e in (1, 3, 2):
            copy_to(b.at[k, 96:288], kv.at[yy, y], r_kv.at[e - 1, yy], ypeer(e))
        kv[yy, y] = b[k, 96:288]
    for e in (1, 3, 2):
        arrived(tokt.at[(y + 4 - e) % 4], r_y.at[e - 1, 4])
    b[4] = project(tokt[...].reshape(128, 1536), 1)
    to_diag = (y + 4 - x) % 4
    used_qt = used[0]
    used[0] += 1

    def text_query():
        return pltpu.make_async_remote_copy(
            src_ref=b.at[4, 0:96], dst_ref=qtraw.at[y], send_sem=send.at[used_qt],
            recv_sem=r_qt.at[to_diag - 1], device_id=at_seq(c, z, x, x), device_id_type=MESH,
        )

    @pl.when(diag)
    def _():
        qtraw[y] = b[4, 0:96]

    @pl.when(jnp.logical_not(diag))
    def _():
        text_query().start()

    for e in (1, 3, 2):
        copy_to(b.at[4, 96:288], kv.at[4, y], r_kv.at[e - 1, 4], ypeer(e))
    kv[4, y] = b[4, 96:288]

    for d in (1, 3, 2):
        arrived(woz.at[d, :, 0:384], r_woz.at[d - 1])
    mine = woz[0, :, pl.ds(pl.multiple_of(z * 384, 128), 384)].astype(F32)
    others = [woz[d, :, 0:384].astype(F32) for d in (1, 2, 3)]
    parts = [mine] + others
    by_z = []
    for zz in range(4):
        block = parts[0]
        for d in (1, 2, 3):
            block = jnp.where((z + 4 - d) % 4 == zz, parts[d], block)
        by_z.append(block)
    here = y * 4 + x
    wov[here] = jnp.concatenate([p[0:24] for p in by_z], axis=0).astype(BF16)
    wot[here] = jnp.concatenate([p[24:48] for p in by_z], axis=0).astype(BF16)
    for d in (1, 3, 2):
        copy_to(wov.at[here], wov.at[here], r_wox.at[d - 1, 0], xpeer(d))
        copy_to(wot.at[here], wot.at[here], r_wox.at[d - 1, 1], xpeer(d))

    def head_norm(raw, gain):
        wide = raw.astype(F32)
        square = jnp.mean(wide * wide, axis=0, keepdims=True)
        return wide * lax.rsqrt(square + 1e-06) * gain

    gq_v, gk_v, gq_t, gk_t = [gains[:, j : j + 1] for j in range(4)]

    def queries(raw, gain):
        return jnp.concatenate(
            [head_norm(raw[128 * h : 128 * h + 128], gain) for h in range(3)], axis=0
        ).astype(BF16)

    for d in (1, 3, 2):
        arrived(qraw.at[(y + d) % 4], r_q.at[d - 1])
    qall[x] = queries(qraw[...].reshape(384, 128), gq_v)
    for d in (1, 3, 2):
        copy_to(qall.at[x], qall.at[x], r_qx.at[d - 1, 0], xpeer(d))
    qt_first = used[0]
    used[0] += 3

    def text_queries(d):
        return pltpu.make_async_remote_copy(
            src_ref=qall.at[4], dst_ref=qall.at[4], send_sem=send.at[qt_first + d - 1],
            recv_sem=r_qx.at[0, 1], device_id=xpeer(d), device_id_type=MESH,
        )

    @pl.when(diag)
    def _():
        for d in (1, 3, 2):
            arrived(qtraw.at[(y + d) % 4], r_qt.at[d - 1])
        qall[4] = queries(qtraw[...].reshape(384, 128), gq_t)
        for d in (1, 3, 2):
            text_queries(d).start()

    for d in (1, 3, 2):
        arrived(wov.at[here], r_wox.at[d - 1, 0])
        arrived(wot.at[here], r_wox.at[d - 1, 1])
    row4 = pl.ds(y * 4, 4)
    for d in (1, 3, 2):
        copy_to(wov.at[row4], wov.at[row4], r_woy.at[d - 1], ypeer(d))
    used_wt = used[0]
    used[0] += 1

    def text_weights():
        return pltpu.make_async_remote_copy(
            src_ref=wot.at[row4], dst_ref=wot.at[row4], send_sem=send.at[used_wt],
            recv_sem=r_woyt.at[to_diag - 1], device_id=at_seq(c, z, x, x), device_id_type=MESH,
        )

    @pl.when(jnp.logical_not(diag))
    def _():
        text_weights().start()

    for ch in range(5):
        for e in (1, 3, 2):
            arrived(kv.at[ch, 0], r_kv.at[e - 1, ch])
        block = kv[ch]
        keys = block[:, 0:96, :].reshape(384, 128)
        vall[:, 128 * ch : 128 * ch + 128] = block[:, 96:192, :].reshape(384, 128)
        for h in range(3):
            turned = head_norm(keys[128 * h : 128 * h + 128], gk_v if ch < 4 else gk_t).T
            kn[h, 128 * ch : 128 * ch + 128, :] = turned.astype(BF16)
    for d in (1, 3, 2):
        arrived(qall.at[(x + 4 - d) % 4], r_qx.at[d - 1, 0])

    @pl.when(jnp.logical_not(diag))
    def _():
        arrived(qall.at[4], r_qx.at[0, 1])

    r = lax.broadcasted_iota(jnp.int32, (128, 128), 0)
    index = (((r % 16) // 4) * 16 + (r // 16) * 4 + x) * 4 + r % 4
    usable = (r < 64) & (index < text_len[c])

    def attend(qc, h):
        scores = (
            jnp.dot(kn[h], qall[qc, 128 * h : 128 * h + 128, :], preferred_element_type=F32)
            * FACTOR
        )
        words = jnp.where(usable, scores[512:640], -1e30)
        scores = jnp.concatenate([scores[0:512], words], axis=0)
        highest = jnp.max(scores, axis=0, keepdims=True)
        weights = jnp.exp(scores - highest)
        total = jnp.sum(weights, axis=0, keepdims=True)
        out = jnp.dot(
            vall[128 * h : 128 * h + 128, :], weights.astype(BF16), preferred_element_type=F32
        )
        osend[qc, 128 * h : 128 * h + 128, :] = (out / total).astype(BF16)
        ssend[qc, h : h + 1, :] = highest
        ssend[qc, 4 + h : 5 + h, :] = total

    for qc in range(5):
        for h in range(3):
            attend(qc, h)
    orecv[x] = osend[x]
    srecv[x] = ssend[x]
    for d in (1, 3, 2):
        copy_to(osend.at[(x + d) % 4], orecv.at[x], r_o.at[d - 1, 0], xpeer(d))
        copy_to(ssend.at[(x + d) % 4], srecv.at[x], r_o.at[d - 1, 1], xpeer(d))
    used_ot = used[0]
    used[0] += 2

    def text_out(i):
        a, bb = ((osend, otrecv), (ssend, strecv))[i]
        return pltpu.make_async_remote_copy(
            src_ref=a.at[4], dst_ref=bb.at[x], send_sem=send.at[used_ot + i],
            recv_sem=r_ot.at[(x + 4 - y) % 4 - 1, i], device_id=at_seq(c, z, y, y),
            device_id_type=MESH,
        )

    @pl.when(diag)
    def _():
        otrecv[x] = osend[4]
        strecv[x] = ssend[4]

    @pl.when(jnp.logical_not(diag))
    def _():
        text_out(0).start()
        text_out(1).start()

    def combine(o, st):
        pieces = []
        for h in range(3):
            top = [st[i, h : h + 1, :] for i in range(4)]
            highest = jnp.maximum(jnp.maximum(top[0], top[1]), jnp.maximum(top[2], top[3]))
            share = [st[i, 4 + h : 5 + h, :] * jnp.exp(top[i] - highest) for i in range(4)]
            total = share[0] + share[1] + share[2] + share[3]
            acc = jnp.zeros((128, 128), F32)
            for i in range(4):
                acc += (share[i] / total) * o[i, 128 * h : 128 * h + 128, :].astype(F32)
            pieces.append(acc)
        return jnp.concatenate(pieces, axis=0).astype(BF16)

    for d in (1, 3, 2):
        arrived(orecv.at[x], r_o.at[d - 1, 0])
        arrived(srecv.at[x], r_o.at[d - 1, 1])
    attended = combine(orecv, srecv)
    for d in (1, 3, 2):
        arrived(wov.at[row4], r_woy.at[d - 1])

    def project_out(weights, values, store):
        out = jnp.dot(weights, values, preferred_element_type=F32)
        for zz in range(4):
            block = jnp.concatenate(
                [out[g * 96 + zz * 24 :][:24] for g in range(16)], axis=0
            )
            store(zz, block.T.astype(BF16))

    def store_video(zz, block):
        for q in range(4):
            pout[q, :, 384 * zz : 384 * zz + 384] = block[32 * q : 32 * q + 32]

    project_out(wov[...].reshape(1536, 384), attended, store_video)
    for d in (1, 3, 2):
        copy_to(pout.at[(z + d) % 4], precv.at[z], r_out.at[d - 1, 0], zpeer(d))

    tp_first = used[0]
    used[0] += 3

    def text_rows(d):
        return pltpu.make_async_remote_copy(
            src_ref=ttout.at[(y + d) % 4], dst_ref=tpart, send_sem=send.at[tp_first + d - 1],
            recv_sem=r_tp.at[0], device_id=ypeer(d), device_id_type=MESH,
        )

    @pl.when(diag)
    def _():
        for d in (1, 3, 2):
            arrived(otrecv.at[x], r_ot.at[d - 1, 0])
            arrived(strecv.at[x], r_ot.at[d - 1, 1])
            arrived(wot.at[row4], r_woyt.at[d - 1])
        attended_text = combine(otrecv, strecv)

        def store_text(zz, block):
            for q in range(4):
                ttout[q, :, 384 * zz : 384 * zz + 384] = block[16 * q : 16 * q + 16]

        project_out(wot[...].reshape(1536, 384), attended_text, store_text)
        for d in (1, 3, 2):
            text_rows(d).start()
        tpart[...] = ttout[y]

    @pl.when(jnp.logical_not(diag))
    def _():
        arrived(tpart, r_tp.at[0])

    rows = tpart[...].astype(F32)
    for q in range(4):
        for j in range(4):
            pack32[4 * j : 4 * j + 4, :] = rows[4 * q : 4 * q + 4, 384 * j : 384 * j + 384]
        tpack[q] = pack32[...].astype(BF16)
    for d in (1, 3, 2):
        copy_to(tpack.at[(z + d) % 4], trecv.at[z], r_out.at[d - 1, 1], zpeer(d))

    total = pout[z].astype(F32)
    for d in (1, 3, 2):
        zz = (z + 4 - d) % 4
        arrived(precv.at[zz], r_out.at[d - 1, 0])
        total += precv[zz].astype(F32)
    projected = total.astype(BF16).astype(F32)
    vout[...] = (zv[z].astype(F32) + mod[2:3, :] * projected).astype(BF16)
    total = tpack[z].astype(F32)
    for d in (1, 3, 2):
        zz = (z + 4 - d) % 4
        arrived(trecv.at[zz], r_out.at[d - 1, 1])
        total += trecv[zz].astype(F32)
    projected = unpack(total.astype(BF16).astype(F32))
    tout[...] = (unpack(zt[z].astype(F32)) + mod[5:6, :] * projected).astype(BF16)

    for op in always:
        op.wait_send()

    @pl.when(diag)
    def _():
        for d in (1, 3, 2):
            text_queries(d).wait_send()
            text_rows(d).wait_send()

    @pl.when(jnp.logical_not(diag))
    def _():
        text_query().wait_send()
        text_weights().wait_send()
        text_out(0).wait_send()
        text_out(1).wait_send()


def body(
    latent_video, text_embed, previous_video, previous_text, noise_blend, modulation,
    w_qkv, w_out, qk_gain, text_len, timestep,
):
    step = timestep[0]
    mod = lax.dynamic_index_in_dim(modulation[0], step, 0, keepdims=False).reshape(6, 1536)
    blend = lax.dynamic_index_in_dim(noise_blend, step, 0, keepdims=False)
    gains = qk_gain.reshape(4, 128).T
    wqkv = w_qkv[0].transpose(0, 1, 3, 2).reshape(144, 1536)
    wout = w_out[0].transpose(0, 2, 1).reshape(48, 1536)
    vm = pl.BlockSpec(memory_space=pltpu.VMEM)
    sm = pl.BlockSpec(memory_space=pltpu.SMEM)
    hbm = pl.BlockSpec(memory_space=pl.ANY)

    def buf(*shape, dtype=BF16):
        return pltpu.VMEM(shape, dtype)

    def sems(*shape):
        return pltpu.SemaphoreType.DMA(shape)

    video, words = pl.pallas_call(
        kernel,
        out_shape=(
            jax.ShapeDtypeStruct((32, 1536), BF16),
            jax.ShapeDtypeStruct((4, 1536), BF16),
        ),
        in_specs=[vm, vm, vm, vm, sm, vm, vm, sm, hbm, hbm],
        out_specs=(vm, vm),
        scratch_shapes=[
            buf(32, 1536), buf(16, 384, dtype=F32), buf(16, 384),
            buf(4, 32, 1536), buf(4, 16, 384), buf(16, 32, 1536), buf(8, 16, 1536),
            buf(4, 144, 1536),
            buf(5, 288, 128), buf(5, 4, 192, 128), buf(4, 96, 128), buf(4, 96, 128),
            buf(5, 384, 128), buf(3, 640, 128), buf(384, 640),
            buf(5, 384, 128), buf(5, 8, 128, dtype=F32),
            buf(4, 384, 128), buf(4, 8, 128, dtype=F32),
            buf(4, 384, 128), buf(4, 8, 128, dtype=F32),
            buf(4, 48, 1536), buf(16, 96, 384), buf(16, 96, 384),
            buf(4, 32, 1536), buf(4, 32, 1536), buf(16, 1536), buf(4, 16, 384),
            buf(4, 16, 384), buf(4, 16, 1536),
            sems(96), sems(4, 2), sems(3), sems(3, 5), sems(3), sems(3), sems(3, 5),
            sems(3, 2), sems(3, 2), sems(3, 2), sems(3), sems(3, 2), sems(3), sems(3),
            sems(3, 2), sems(1), sems(2),
        ],
        compiler_params=pltpu.CompilerParams(
            collective_id=0, has_side_effects=True, vmem_limit_bytes=48 << 20
        ),
    )(
        latent_video, text_embed, previous_video[0], previous_text[0], blend, mod, gains,
        text_len, wqkv, wout,
    )
    return video[None], words[None]


def solution(mesh):
    placed = (
        P("seq", None),
        P("seq", None),
        P("comp", "seq", None),
        P("comp", "seq", None),
        P(),
        P("comp", None, None, None, None),
        P("comp", None, None, None, "seq"),
        P("comp", None, None, "seq"),
        P("comp", None, None, None),
        P(),
        P(),
    )
    return jax.shard_map(
        body,
        mesh=mesh,
        in_specs=placed,
        out_specs=(P("comp", "seq", None), P("comp", "seq", None)),
        check_vma=False,
    )
```

```python
import math

import jax
import jax.numpy as jnp
from jax import lax
from jax.experimental import pallas as pl
from jax.experimental.pallas import tpu as pltpu
from jax.sharding import PartitionSpec as P

HEAD_DIM = 128
F32, BF16 = jnp.float32, jnp.bfloat16
MESH = pl.DeviceIdType.MESH
FACTOR = 1.0 / math.sqrt(HEAD_DIM)


def kernel(
    timestep, text_len, latent, text, prev_v, prev_t, blend_hbm, mod_hbm, gains_hbm, wqkv, wout,
    vout, tout,
    latent_v, text_v, old_v, old_t, blend, mod_all, gains, mod, turned,
    vsend, pack32, tsend, zv, zt, tokv, tokt, wq, packed,
    b, kv, qraw, qtraw, qall, kn, vall,
    osend, ssend, orecv, srecv, otrecv, strecv,
    wo, att, tall, tpk, pout, precv,
    send, r_z, r_w, r_y, r_q, r_qt, r_kv, r_qx, r_o, r_ot,
    r_wo, r_wox, r_att, r_attt, r_out, loc,
):
    c = lax.axis_index("comp")
    s = lax.axis_index("seq")
    odd = c % 2
    z, a0, a1 = s // 16, (s // 4) % 4, s % 4
    y = a0 + odd * (a1 - a0)
    x = a1 + odd * (a0 - a1)
    diag = y == x

    def at_seq(zz, yy, xx):
        return (c, zz * 16 + yy * (4 - 3 * odd) + xx * (1 + 3 * odd))

    def ypeer(d):
        return at_seq(z, (y + d) % 4, x)

    def zypeer(dz, dy):
        return at_seq((z + dz) % 4, (y + dy) % 4, x)

    def xpeer(d):
        return at_seq(z, y, (x + d) % 4)

    used = [0]
    always, on_diag, off_diag = [], [], []

    def copy_to(src, dst, recv, device, group=None):
        op = pltpu.make_async_remote_copy(
            src_ref=src, dst_ref=dst, send_sem=send.at[used[0]], recv_sem=recv,
            device_id=device, device_id_type=MESH,
        )
        used[0] += 1
        op.start()
        (always if group is None else group).append(op)

    def arrived(dst, recv):
        pltpu.make_async_remote_copy(
            src_ref=dst, dst_ref=dst, send_sem=send.at[0], recv_sem=recv,
            device_id=xpeer(1), device_id_type=MESH,
        ).wait_recv()

    nextc, prevc = (c + 1) % 4, (c + 3) % 4
    barrier = pltpu.get_barrier_semaphore()
    for d in range(4):
        pl.semaphore_signal(barrier, inc=1, device_id=(prevc, (s + 16 * d) % 64), device_id_type=MESH)
    for dz in range(4):
        for dy in range(4):
            if dz or dy:
                pl.semaphore_signal(barrier, inc=1, device_id=zypeer(dz, dy), device_id_type=MESH)
    for d in (1, 2, 3):
        pl.semaphore_signal(barrier, inc=1, device_id=xpeer(d), device_id_type=MESH)

    loads = [
        pltpu.make_async_copy(a, bb, loc.at[i])
        for i, (a, bb) in enumerate(
            (
                (latent, latent_v), (prev_v, old_v), (text, text_v), (prev_t, old_t),
                (blend_hbm, blend), (mod_hbm, mod_all), (gains_hbm, gains), (wqkv, wq.at[x]),
            )
        )
    ]
    for op in loads:
        op.start()
    for op in loads[:7]:
        op.wait()

    step = timestep[0]
    lane = lax.broadcasted_iota(jnp.int32, (2, 50), 1)
    pair = jnp.sum(jnp.where(lane == step, blend[...], 0.0), axis=1, keepdims=True)
    last = c == 3
    old = old_v[...]
    mixed = (pair[0:1] * latent_v[...].astype(F32) + pair[1:2] * old.astype(F32)).astype(BF16)
    vsend[...] = jnp.where(last, mixed, old)
    words = jnp.where(last, text_v[...], old_t[...]).astype(F32)
    for j in range(4):
        pack32[4 * j : 4 * j + 4, :] = words[:, 384 * j : 384 * j + 384]
    tsend[...] = pack32[...].astype(BF16)
    tokt[4:8] = jnp.zeros((4, 16, 1536), BF16)
    for st in range(2):
        for k in range(3):
            mod[3 * st + k : 3 * st + k + 1, :] = mod_all[step, k, st : st + 1, :]
        for k in range(2):
            turned[2 * st + k] = jnp.broadcast_to(gains[st, k : k + 1, :], (128, 128)).T

    pl.semaphore_wait(barrier, 22)

    for d in (0, 1, 3, 2):
        copy_to(vsend, zv.at[z], r_z.at[d, 0], (nextc, (s + 16 * d) % 64))
    for d in (0, 1, 3, 2):
        copy_to(tsend, zt.at[z], r_z.at[d, 1], (nextc, (s + 16 * d) % 64))
    for i, part in enumerate((pl.ds(0, 80), pl.ds(80, 64))):
        for d in (1, 3, 2):
            copy_to(wqkv.at[part], wq.at[x, part], r_w.at[d - 1, i], xpeer(d))

    def normed(wide, stream):
        center = wide - jnp.mean(wide, axis=-1, keepdims=True)
        spread = jnp.mean(center * center, axis=-1, keepdims=True)
        shift = mod[3 * stream : 3 * stream + 1, :]
        scale = mod[3 * stream + 1 : 3 * stream + 2, :]
        return (center * lax.rsqrt(spread + 1e-06) * (1.0 + scale) + shift).astype(BF16)

    def unpack(packed):
        return jnp.concatenate([packed[4 * j : 4 * j + 4, :] for j in range(4)], axis=1)

    for d in (0, 1, 3, 2):
        zz = (z + 4 - d) % 4
        arrived(zv.at[zz], r_z.at[d, 0])
        slot = y * 4 + zz
        tokv[slot] = normed(zv[zz].astype(F32), 0)
        for e in (1, 3, 2):
            copy_to(tokv.at[slot], tokv.at[slot], r_y.at[e - 1, d], ypeer(e))
    for d in (0, 1, 3, 2):
        arrived(zt.at[(z + 4 - d) % 4], r_z.at[d, 1])
    rows = jnp.concatenate([unpack(zt[j].astype(F32)) for j in range(4)], axis=0)
    tokt[y] = normed(rows, 1)
    for e in (1, 3, 2):
        copy_to(tokt.at[y], tokt.at[y], r_y.at[e - 1, 4], ypeer(e))

    def wo_part(d):
        return wout.at[:, pl.ds(pl.multiple_of(((z + d) % 4) * 384, 128), 384)]

    for d in (1, 3, 2):
        copy_to(wo_part(d), wo.at[x, y], r_wo.at[y], at_seq((z + d) % 4, z, x))
    wo_slot = used[0]
    used[0] += 1

    def wo_near():
        return pltpu.make_async_remote_copy(
            src_ref=wo_part(0), dst_ref=wo.at[x, y], send_sem=send.at[wo_slot],
            recv_sem=r_wo.at[y], device_id=at_seq(z, z, x), device_id_type=MESH,
        )

    def wo_own():
        return pltpu.make_async_copy(wo_part(0), wo.at[x, y], loc.at[8])

    @pl.when(y == z)
    def _():
        wo_own().start()

    @pl.when(y != z)
    def _():
        wo_near().start()

    loads[7].wait()

    def regroup(stream):
        wide = [wq[xx, 72 * stream : 72 * stream + 72].astype(F32) for xx in range(4)]
        packed[stream] = jnp.concatenate(
            [wide[xx][24 * j : 24 * j + 24] for j in range(3) for xx in range(4)], axis=0
        ).astype(BF16)

    def project(tokens, stream):
        return lax.dot_general(
            packed[stream], tokens, (((1,), (1,)), ((), ())), preferred_element_type=F32
        ).astype(BF16)

    for d in (1, 3, 2):
        arrived(wq.at[(x + 4 - d) % 4, pl.ds(0, 80)], r_w.at[d - 1, 0])
    regroup(0)
    order = (0, 1, 3, 2)
    for k, d in enumerate(order):
        yy = (y + 4 - d) % 4
        if d:
            for dz in range(4):
                arrived(tokv.at[yy * 4 + dz], r_y.at[d - 1, dz])
        b[k] = project(tokv[pl.ds(yy * 4, 4)].reshape(128, 1536), 0)
        if d:
            copy_to(b.at[k, 0:96], qraw.at[y], r_q.at[d - 1], ypeer(4 - d))
        else:
            qraw[y] = b[k, 0:96]
    for k, d in enumerate(order):
        yy = (y + 4 - d) % 4
        for e in (1, 3, 2):
            copy_to(b.at[k, 96:288], kv.at[yy, y], r_kv.at[e - 1, yy], ypeer(e))
        kv[yy, y] = b[k, 96:288]
    for d in (1, 3, 2):
        arrived(wq.at[(x + 4 - d) % 4, pl.ds(80, 64)], r_w.at[d - 1, 1])
    regroup(1)
    for e in (1, 3, 2):
        arrived(tokt.at[(y + 4 - e) % 4], r_y.at[e - 1, 4])
    b[4] = project(tokt[...].reshape(128, 1536), 1)
    to_diag = (y + 4 - x) % 4
    used_qt = used[0]
    used[0] += 1

    def text_query():
        return pltpu.make_async_remote_copy(
            src_ref=b.at[4, 0:96], dst_ref=qtraw.at[y], send_sem=send.at[used_qt],
            recv_sem=r_qt.at[to_diag - 1], device_id=at_seq(z, x, x), device_id_type=MESH,
        )

    @pl.when(diag)
    def _():
        qtraw[y] = b[4, 0:96]

    @pl.when(jnp.logical_not(diag))
    def _():
        text_query().start()

    for e in (1, 3, 2):
        copy_to(b.at[4, 96:288], kv.at[4, y], r_kv.at[e - 1, 4], ypeer(e))
    kv[4, y] = b[4, 96:288]

    def natural(groups):
        straight = [groups[g] for g in range(16)]
        crossed = [groups[(g % 4) * 4 + g // 4] for g in range(16)]
        return jnp.where(
            odd == 1, jnp.concatenate(crossed, axis=0), jnp.concatenate(straight, axis=0)
        )

    def by_rows(slabs):
        wide = [slabs[yy].astype(F32) for yy in range(4)]
        return natural([wide[g // 4][24 * (g % 4) : 24 * (g % 4) + 24] for g in range(16)])

    def head_norm(raw, gain):
        square = jnp.mean(raw * raw, axis=0, keepdims=True)
        return raw * lax.rsqrt(square + 1e-06) * gain

    gq_v, gk_v, gq_t, gk_t = [turned[j] for j in range(4)]

    def queries(raw, gain):
        return jnp.concatenate(
            [head_norm(raw[128 * h : 128 * h + 128], gain) for h in range(3)], axis=0
        ).astype(BF16)

    for d in (1, 3, 2):
        arrived(qraw.at[(y + d) % 4], r_q.at[d - 1])
    qall[x] = queries(by_rows(qraw), gq_v)
    for d in (1, 3, 2):
        copy_to(qall.at[x], qall.at[x], r_qx.at[d - 1, 0], xpeer(d))
    qt_first = used[0]
    used[0] += 3

    def text_queries(d):
        return pltpu.make_async_remote_copy(
            src_ref=qall.at[4], dst_ref=qall.at[4], send_sem=send.at[qt_first + d - 1],
            recv_sem=r_qx.at[0, 1], device_id=xpeer(d), device_id_type=MESH,
        )

    @pl.when(diag)
    def _():
        for d in (1, 3, 2):
            arrived(qtraw.at[(y + d) % 4], r_qt.at[d - 1])
        qall[4] = queries(by_rows(qtraw), gq_t)
        for d in (1, 3, 2):
            text_queries(d).start()

    for ch in range(5):
        for e in (1, 3, 2):
            arrived(kv.at[ch, 0], r_kv.at[e - 1, ch])
        keys = by_rows([kv[ch, yy, 0:96] for yy in range(4)])
        values = by_rows([kv[ch, yy, 96:192] for yy in range(4)])
        vall[:, 128 * ch : 128 * ch + 128] = values.astype(BF16)
        for h in range(3):
            key = head_norm(keys[128 * h : 128 * h + 128], gk_v if ch < 4 else gk_t).T
            kn[h, 128 * ch : 128 * ch + 128, :] = key.astype(BF16)
    @pl.when(y == z)
    def _():
        wo_own().wait()

    @pl.when(y != z)
    def _():
        arrived(wo.at[x, y], r_wo.at[y])

    for d in (1, 2, 3):
        arrived(wo.at[x, (y + d) % 4], r_wo.at[(y + d) % 4])

    for d in (1, 3, 2):
        copy_to(wo.at[x], wo.at[x], r_wox.at[d - 1], xpeer(d))

    for d in (1, 3, 2):
        arrived(qall.at[(x + 4 - d) % 4], r_qx.at[d - 1, 0])

    @pl.when(jnp.logical_not(diag))
    def _():
        arrived(qall.at[4], r_qx.at[0, 1])

    r = lax.broadcasted_iota(jnp.int32, (128, 128), 0)
    place = (r // 16) * (4 - 3 * odd) + x * (1 + 3 * odd)
    index = (((r % 16) // 4) * 16 + place) * 4 + r % 4
    usable = (r < 64) & (index < text_len[c])

    def attend(qc, h):
        scores = (
            jnp.dot(kn[h], qall[qc, 128 * h : 128 * h + 128, :], preferred_element_type=F32)
            * FACTOR
        )
        words = jnp.where(usable, scores[512:640], -1e30)
        scores = jnp.concatenate([scores[0:512], words], axis=0)
        highest = jnp.max(scores, axis=0, keepdims=True)
        weights = jnp.exp(scores - highest)
        total = jnp.sum(weights, axis=0, keepdims=True)
        out = jnp.dot(
            vall[128 * h : 128 * h + 128, :], weights.astype(BF16), preferred_element_type=F32
        )
        osend[h, qc] = (out / total).astype(BF16)
        ssend[h, qc, 0:1, :] = highest
        ssend[h, qc, 1:2, :] = total

    ot_first = used[0]
    used[0] += 6
    at_first = used[0]
    used[0] += 9

    def text_out(h, i):
        a, bb = ((osend, otrecv), (ssend, strecv))[i]
        return pltpu.make_async_remote_copy(
            src_ref=a.at[h, 4], dst_ref=bb.at[h, x], send_sem=send.at[ot_first + 2 * h + i],
            recv_sem=r_ot.at[(x + 4 - y) % 4 - 1, h, i], device_id=at_seq(z, y, y),
            device_id_type=MESH,
        )

    def text_att(h, d):
        part = att.at[4, pl.ds(128 * h, 128)]
        return pltpu.make_async_remote_copy(
            src_ref=part, dst_ref=part, send_sem=send.at[at_first + 3 * h + d - 1],
            recv_sem=r_attt.at[h], device_id=ypeer(d), device_id_type=MESH,
        )

    def attend_head(h):
        for d in (2, 1, 3):
            qc = (x + d) % 4
            attend(qc, h)
            copy_to(osend.at[h, qc], orecv.at[h, x], r_o.at[d - 1, h, 0], xpeer(d))
            copy_to(ssend.at[h, qc], srecv.at[h, x], r_o.at[d - 1, h, 1], xpeer(d))
        attend(4, h)

        @pl.when(diag)
        def _():
            otrecv[h, x] = osend[h, 4]
            strecv[h, x] = ssend[h, 4]

        @pl.when(jnp.logical_not(diag))
        def _():
            text_out(h, 0).start()
            text_out(h, 1).start()

        attend(x, h)
        orecv[h, x] = osend[h, x]
        srecv[h, x] = ssend[h, x]

    def combine(o, st, h):
        top = [st[h, i, 0:1, :] for i in range(4)]
        highest = jnp.maximum(jnp.maximum(top[0], top[1]), jnp.maximum(top[2], top[3]))
        share = [st[h, i, 1:2, :] * jnp.exp(top[i] - highest) for i in range(4)]
        total = share[0] + share[1] + share[2] + share[3]
        acc = jnp.zeros((128, 128), F32)
        for i in range(4):
            acc += (share[i] / total) * o[h, i].astype(F32)
        return acc.astype(BF16)

    def combine_head(h):
        part = pl.ds(128 * h, 128)
        for d in (1, 3, 2):
            arrived(orecv.at[h, x], r_o.at[d - 1, h, 0])
            arrived(srecv.at[h, x], r_o.at[d - 1, h, 1])
        att[y, part] = combine(orecv, srecv, h)
        for d in (1, 3, 2):
            copy_to(att.at[y, part], att.at[y, part], r_att.at[d - 1, h], ypeer(d))

        @pl.when(diag)
        def _():
            for d in (1, 3, 2):
                arrived(otrecv.at[h, x], r_ot.at[d - 1, h, 0])
                arrived(strecv.at[h, x], r_ot.at[d - 1, h, 1])
            att[4, part] = combine(otrecv, strecv, h)
            for d in (1, 3, 2):
                text_att(h, d).start()

    attend_head(0)
    attend_head(1)
    combine_head(0)
    attend_head(2)
    combine_head(1)
    combine_head(2)
    for d in (1, 3, 2):
        arrived(wo.at[x], r_wox.at[d - 1])
    weights_out = wo[...].reshape(768, 384)

    def project_out(values, stream):
        out = jnp.dot(weights_out, values, preferred_element_type=F32)
        return natural(
            [
                out[(xx * 4 + yy) * 48 + stream * 24 :][:24]
                for yy in range(4)
                for xx in range(4)
            ]
        ).T

    def video_block(slot):
        block = project_out(att[slot], 0).astype(BF16)
        for q in range(4):
            for j in range(3):
                pout[slot, q, 32 * j : 32 * j + 32, :] = block[
                    32 * q : 32 * q + 32, 128 * j : 128 * j + 128
                ]

    video_block(y)

    @pl.when(jnp.logical_not(diag))
    def _():
        for h in range(3):
            arrived(att.at[4, pl.ds(128 * h, 128)], r_attt.at[h])

    tall[...] = project_out(att[4], 1)
    for yy in range(4):
        for q in range(4):
            for j in range(3):
                pack32[4 * j : 4 * j + 4, 0:128] = tall[
                    16 * yy + 4 * q : 16 * yy + 4 * q + 4, 128 * j : 128 * j + 128
                ]
            tpk[yy, q] = pack32[:, 0:128].astype(BF16)

    for dy in (0, 1, 3, 2):
        slot = (y + dy) % 4
        if dy:
            for h in range(3):
                arrived(att.at[slot, pl.ds(128 * h, 128)], r_att.at[3 - dy, h])
            video_block(slot)
        for q in range(4):
            pout[slot, q, 96:112, :] = tpk[slot, q]
        for dz in (2, 1, 3, 0):
            if dy or dz:
                copy_to(
                    pout.at[slot, (z + dz) % 4], precv.at[z, y], r_out.at[dz, dy], zypeer(dz, dy)
                )
            else:
                precv[z, y] = pout[slot, z]

    for dy in (0, 1, 3, 2):
        for dz in (0, 1, 3, 2):
            if dy or dz:
                arrived(precv.at[z, y], r_out.at[dz, dy])
    for yy in range(4):
        total = precv[0, yy].astype(F32)
        for zz in range(1, 4):
            total += precv[zz, yy].astype(F32)
        total = total.astype(BF16).astype(F32)
        for j in range(3):
            at = pl.ds(384 * yy + 128 * j, 128)
            vout[:, at] = (
                zv[z, :, at].astype(F32) + mod[2:3, at] * total[32 * j : 32 * j + 32]
            ).astype(BF16)
            own = zt[z, 4 * yy : 4 * yy + 4, 128 * j : 128 * j + 128].astype(F32)
            tout[:, at] = (own + mod[5:6, at] * total[96 + 4 * j : 100 + 4 * j]).astype(BF16)

    for op in always:
        op.wait_send()

    @pl.when(y != z)
    def _():
        wo_near().wait_send()

    @pl.when(diag)
    def _():
        for d in (1, 3, 2):
            text_queries(d).wait_send()
            for h in range(3):
                text_att(h, d).wait_send()

    @pl.when(jnp.logical_not(diag))
    def _():
        text_query().wait_send()
        for h in range(3):
            text_out(h, 0).wait_send()
            text_out(h, 1).wait_send()


def body(
    latent_video, text_embed, previous_video, previous_text, noise_blend, modulation,
    w_qkv, w_out, qk_gain, text_len, timestep,
):
    blend = noise_blend.T
    mod = modulation[0].transpose(0, 2, 1, 3)
    gains = qk_gain[0]
    wqkv = w_qkv[0].transpose(0, 1, 3, 2).reshape(144, 1536)
    wout = w_out[0].transpose(0, 2, 1).reshape(48, 1536)
    vm = pl.BlockSpec(memory_space=pltpu.VMEM)
    sm = pl.BlockSpec(memory_space=pltpu.SMEM)
    hbm = pl.BlockSpec(memory_space=pltpu.HBM)

    def buf(*shape, dtype=BF16):
        return pltpu.VMEM(shape, dtype)

    def sems(*shape):
        return pltpu.SemaphoreType.DMA(shape)

    video, words = pl.pallas_call(
        kernel,
        out_shape=(
            jax.ShapeDtypeStruct((32, 1536), BF16),
            jax.ShapeDtypeStruct((4, 1536), BF16),
        ),
        in_specs=[sm, sm] + [hbm] * 9,
        out_specs=(vm, vm),
        scratch_shapes=[
            buf(32, 1536), buf(4, 1536), buf(32, 1536), buf(4, 1536), buf(2, 50, dtype=F32),
            buf(50, 3, 2, 1536, dtype=F32), buf(2, 2, 128, dtype=F32), buf(8, 1536, dtype=F32),
            buf(4, 128, 128, dtype=F32),
            buf(32, 1536), buf(16, 384, dtype=F32), buf(16, 384),
            buf(4, 32, 1536), buf(4, 16, 384), buf(16, 32, 1536), buf(8, 16, 1536),
            buf(4, 144, 1536), buf(2, 288, 1536),
            buf(5, 288, 128), buf(5, 4, 192, 128), buf(4, 96, 128), buf(4, 96, 128),
            buf(5, 384, 128), buf(3, 640, 128), buf(384, 640),
            buf(3, 5, 128, 128), buf(3, 5, 8, 128, dtype=F32),
            buf(3, 4, 128, 128), buf(3, 4, 8, 128, dtype=F32),
            buf(3, 4, 128, 128), buf(3, 4, 8, 128, dtype=F32),
            buf(4, 4, 48, 384), buf(5, 384, 128), buf(128, 384, dtype=F32), buf(4, 4, 16, 128),
            buf(4, 4, 112, 128), buf(4, 4, 112, 128),
            sems(144), sems(4, 2), sems(3, 2), sems(3, 5), sems(3), sems(3), sems(3, 5),
            sems(3, 2), sems(3, 3, 2), sems(3, 3, 2), sems(4), sems(3), sems(3, 3), sems(3),
            sems(4, 4), sems(9),
        ],
        compiler_params=pltpu.CompilerParams(
            collective_id=0, has_side_effects=True, vmem_limit_bytes=62 << 20
        ),
    )(
        timestep, text_len, latent_video, text_embed, previous_video[0], previous_text[0],
        blend, mod, gains, wqkv, wout,
    )
    return video[None], words[None]


def solution(mesh):
    placed = (
        P("seq", None),
        P("seq", None),
        P("comp", "seq", None),
        P("comp", "seq", None),
        P(),
        P("comp", None, None, None, None),
        P("comp", None, None, None, "seq"),
        P("comp", None, None, "seq"),
        P("comp", None, None, None),
        P(),
        P(),
    )
    return jax.shard_map(
        body,
        mesh=mesh,
        in_specs=placed,
        out_specs=(P("comp", "seq", None), P("comp", "seq", None)),
        check_vma=False,
    )
```

```python
import math

import jax
import jax.numpy as jnp
from jax import lax
from jax.experimental import pallas as pl
from jax.experimental.pallas import tpu as pltpu
from jax.sharding import PartitionSpec as P

HEAD_DIM = 128
F32, BF16 = jnp.float32, jnp.bfloat16
MESH = pl.DeviceIdType.MESH
FACTOR = 1.0 / math.sqrt(HEAD_DIM)


def kernel(
    timestep, text_len, latent, text, prev_v, prev_t, blend_hbm, mod_hbm, gains_hbm, wqkv, wout,
    vout, tout,
    latent_v, text_v, old_v, old_t, blend, mod_all, gains, mod, turned,
    vsend, pack32, tsend, zv, zt, tokv, tokt, wq, packed,
    b, kv, qraw, qtraw, qall, kn, vall,
    osend, ssend, orecv, srecv, otrecv, strecv,
    wo, att, tall, tpk, pout, precv,
    send, r_z, r_w, r_y, r_q, r_qt, r_kv, r_qx, r_o, r_ot,
    r_wo, r_wox, r_att, r_attt, r_out, loc,
):
    c = lax.axis_index("comp")
    s = lax.axis_index("seq")
    odd = c % 2
    z, a0, a1 = s // 16, (s // 4) % 4, s % 4
    y = a0 + odd * (a1 - a0)
    x = a1 + odd * (a0 - a1)
    diag = y == x

    def at_seq(zz, yy, xx):
        return (c, zz * 16 + yy * (4 - 3 * odd) + xx * (1 + 3 * odd))

    def ypeer(d):
        return at_seq(z, (y + d) % 4, x)

    def zypeer(dz, dy):
        return at_seq((z + dz) % 4, (y + dy) % 4, x)

    def xpeer(d):
        return at_seq(z, y, (x + d) % 4)

    used = [0]
    always, on_diag, off_diag = [], [], []

    def copy_to(src, dst, recv, device, group=None):
        op = pltpu.make_async_remote_copy(
            src_ref=src, dst_ref=dst, send_sem=send.at[used[0]], recv_sem=recv,
            device_id=device, device_id_type=MESH,
        )
        used[0] += 1
        op.start()
        (always if group is None else group).append(op)

    def arrived(dst, recv):
        pltpu.make_async_remote_copy(
            src_ref=dst, dst_ref=dst, send_sem=send.at[0], recv_sem=recv,
            device_id=xpeer(1), device_id_type=MESH,
        ).wait_recv()

    nextc, prevc = (c + 1) % 4, (c + 3) % 4
    barrier = pltpu.get_barrier_semaphore()
    for d in range(4):
        pl.semaphore_signal(barrier, inc=1, device_id=(prevc, (s + 16 * d) % 64), device_id_type=MESH)
    for dz in range(4):
        for dy in range(4):
            if dz or dy:
                pl.semaphore_signal(barrier, inc=1, device_id=zypeer(dz, dy), device_id_type=MESH)
    for d in (1, 2, 3):
        pl.semaphore_signal(barrier, inc=1, device_id=xpeer(d), device_id_type=MESH)

    loads = [
        pltpu.make_async_copy(a, bb, loc.at[i])
        for i, (a, bb) in enumerate(
            (
                (latent, latent_v), (prev_v, old_v), (text, text_v), (prev_t, old_t),
                (blend_hbm, blend), (mod_hbm, mod_all), (gains_hbm, gains), (wqkv, wq.at[x]),
            )
        )
    ]
    for op in loads:
        op.start()
    for op in loads[:5]:
        op.wait()

    step = timestep[0]
    lane = lax.broadcasted_iota(jnp.int32, (2, 50), 1)
    pair = jnp.sum(jnp.where(lane == step, blend[...], 0.0), axis=1, keepdims=True)
    last = c == 3
    old = old_v[...]
    mixed = (pair[0:1] * latent_v[...].astype(F32) + pair[1:2] * old.astype(F32)).astype(BF16)
    vsend[...] = jnp.where(last, mixed, old)
    words = jnp.where(last, text_v[...], old_t[...]).astype(F32)
    for j in range(4):
        pack32[4 * j : 4 * j + 4, :] = words[:, 384 * j : 384 * j + 384]
    tsend[...] = pack32[...].astype(BF16)
    tokt[4:8] = jnp.zeros((4, 16, 1536), BF16)
    pl.semaphore_wait(barrier, 22)

    for d in (2, 1, 3, 0):
        copy_to(tsend, zt.at[z], r_z.at[d, 1], (nextc, (s + 16 * d) % 64))
    for d in (0, 1, 3, 2):
        copy_to(vsend, zv.at[z], r_z.at[d, 0], (nextc, (s + 16 * d) % 64))
    for i, part in enumerate((pl.ds(0, 80), pl.ds(80, 64))):
        for d in (1, 3, 2):
            copy_to(wqkv.at[part], wq.at[x, part], r_w.at[d - 1, i], xpeer(d))

    for op in loads[5:7]:
        op.wait()
    for st in range(2):
        for k in range(3):
            mod[3 * st + k : 3 * st + k + 1, :] = mod_all[step, k, st : st + 1, :]
        for k in range(2):
            turned[2 * st + k] = jnp.broadcast_to(gains[st, k : k + 1, :], (128, 128)).T

    def normed(wide, stream):
        center = wide - jnp.mean(wide, axis=-1, keepdims=True)
        spread = jnp.mean(center * center, axis=-1, keepdims=True)
        shift = mod[3 * stream : 3 * stream + 1, :]
        scale = mod[3 * stream + 1 : 3 * stream + 2, :]
        return (center * lax.rsqrt(spread + 1e-06) * (1.0 + scale) + shift).astype(BF16)

    def unpack(packed):
        return jnp.concatenate([packed[4 * j : 4 * j + 4, :] for j in range(4)], axis=1)

    def norm_piece(d):
        zz = (z + 4 - d) % 4
        arrived(zv.at[zz], r_z.at[d, 0])
        slot = zz * 4 + y
        tokv[slot] = normed(zv[zz].astype(F32), 0)
        for e in (1, 3, 2):
            copy_to(tokv.at[slot], tokv.at[slot], r_y.at[e - 1, d], ypeer(e))

    norm_piece(0)
    for d in (0, 1, 3, 2):
        arrived(zt.at[(z + 4 - d) % 4], r_z.at[d, 1])
    rows = jnp.concatenate([unpack(zt[j].astype(F32)) for j in range(4)], axis=0)
    tokt[y] = normed(rows, 1)
    for e in (1, 3, 2):
        copy_to(tokt.at[y], tokt.at[y], r_y.at[e - 1, 4], ypeer(e))
    norm_piece(1)
    norm_piece(3)

    loads[7].wait()

    def regroup(stream):
        wide = [wq[xx, 72 * stream : 72 * stream + 72].astype(F32) for xx in range(4)]
        packed[stream] = jnp.concatenate(
            [wide[xx][24 * j : 24 * j + 24] for j in range(3) for xx in range(4)], axis=0
        ).astype(BF16)

    def project(tokens, stream):
        return lax.dot_general(
            packed[stream], tokens, (((1,), (1,)), ((), ())), preferred_element_type=F32
        ).astype(BF16)

    def natural(groups):
        straight = [groups[g] for g in range(16)]
        crossed = [groups[(g % 4) * 4 + g // 4] for g in range(16)]
        return jnp.where(
            odd == 1, jnp.concatenate(crossed, axis=0), jnp.concatenate(straight, axis=0)
        )

    def by_rows(slabs):
        wide = [slabs[yy].astype(F32) for yy in range(4)]
        return natural([wide[g // 4][24 * (g % 4) : 24 * (g % 4) + 24] for g in range(16)])

    def head_norm(raw, gain):
        square = jnp.mean(raw * raw, axis=0, keepdims=True)
        return raw * lax.rsqrt(square + 1e-06) * gain

    gq_v, gk_v, gq_t, gk_t = [turned[j] for j in range(4)]

    def queries(raw, gain):
        return jnp.concatenate(
            [head_norm(raw[128 * h : 128 * h + 128], gain) for h in range(3)], axis=0
        ).astype(BF16)

    def set_keys(ch):
        for e in (1, 3, 2):
            arrived(kv.at[ch, 0], r_kv.at[e - 1, ch])
        keys = by_rows([kv[ch, yy, 0:96] for yy in range(4)])
        values = by_rows([kv[ch, yy, 96:192] for yy in range(4)])
        vall[:, 128 * ch : 128 * ch + 128] = values.astype(BF16)
        for h in range(3):
            key = head_norm(keys[128 * h : 128 * h + 128], gk_v if ch < 4 else gk_t)
            kn[h, 128 * ch : 128 * ch + 128, :] = key.astype(BF16).T

    query_first = used[0]
    used[0] += 4

    def query_send(k, zz):
        return pltpu.make_async_remote_copy(
            src_ref=b.at[k, 0:96], dst_ref=qraw.at[y], send_sem=send.at[query_first + k],
            recv_sem=r_q.at[y], device_id=at_seq(z, zz, x), device_id_type=MESH,
        )

    order = (0, 1, 3, 2)

    def video_chunk(k):
        d = order[k]
        zz = (z + 4 - d) % 4
        for e in (1, 3, 2):
            arrived(tokv.at[zz * 4 + (y + 4 - e) % 4], r_y.at[e - 1, d])
        b[k] = project(tokv[pl.ds(zz * 4, 4)].reshape(128, 1536), 0)

        @pl.when(zz == y)
        def _():
            qraw[y] = b[k, 0:96]

        @pl.when(zz != y)
        def _():
            query_send(k, zz).start()

        for e in (1, 3, 2):
            copy_to(b.at[k, 96:288], kv.at[k, y], r_kv.at[e - 1, k], ypeer(e))
        kv[k, y] = b[k, 96:288]

    for d in (1, 3, 2):
        arrived(wq.at[(x + 4 - d) % 4, pl.ds(0, 80)], r_w.at[d - 1, 0])
    regroup(0)
    video_chunk(0)
    norm_piece(2)
    def wo_part(d):
        return wout.at[:, pl.ds(pl.multiple_of(((z + d) % 4) * 384, 128), 384)]

    for d in (1, 3, 2):
        copy_to(wo_part(d), wo.at[x, y], r_wo.at[y], at_seq((z + d) % 4, z, x))
    wo_slot = used[0]
    used[0] += 1

    def wo_near():
        return pltpu.make_async_remote_copy(
            src_ref=wo_part(0), dst_ref=wo.at[x, y], send_sem=send.at[wo_slot],
            recv_sem=r_wo.at[y], device_id=at_seq(z, z, x), device_id_type=MESH,
        )

    def wo_own():
        return pltpu.make_async_copy(wo_part(0), wo.at[x, y], loc.at[8])

    @pl.when(y == z)
    def _():
        wo_own().start()

    @pl.when(y != z)
    def _():
        wo_near().start()

    video_chunk(1)
    video_chunk(2)
    for d in (1, 3, 2):
        arrived(wq.at[(x + 4 - d) % 4, pl.ds(80, 64)], r_w.at[d - 1, 1])
    regroup(1)
    for e in (1, 3, 2):
        arrived(tokt.at[(y + 4 - e) % 4], r_y.at[e - 1, 4])
    b[4] = project(tokt[...].reshape(128, 1536), 1)
    to_diag = (y + 4 - x) % 4
    used_qt = used[0]
    used[0] += 1

    def text_query():
        return pltpu.make_async_remote_copy(
            src_ref=b.at[4, 0:96], dst_ref=qtraw.at[y], send_sem=send.at[used_qt],
            recv_sem=r_qt.at[to_diag - 1], device_id=at_seq(z, x, x), device_id_type=MESH,
        )

    @pl.when(diag)
    def _():
        qtraw[y] = b[4, 0:96]

    @pl.when(jnp.logical_not(diag))
    def _():
        text_query().start()

    for e in (1, 3, 2):
        copy_to(b.at[4, 96:288], kv.at[4, y], r_kv.at[e - 1, 4], ypeer(e))
    kv[4, y] = b[4, 96:288]

    set_keys(0)
    video_chunk(3)
    for d in (1, 3, 2):
        arrived(qraw.at[(y + d) % 4], r_q.at[(y + d) % 4])
    qall[x] = queries(by_rows(qraw), gq_v)
    for d in (1, 3, 2):
        copy_to(qall.at[x], qall.at[x], r_qx.at[d - 1, 0], xpeer(d))
    qt_first = used[0]
    used[0] += 3

    def text_queries(d):
        return pltpu.make_async_remote_copy(
            src_ref=qall.at[4], dst_ref=qall.at[4], send_sem=send.at[qt_first + d - 1],
            recv_sem=r_qx.at[0, 1], device_id=xpeer(d), device_id_type=MESH,
        )

    @pl.when(diag)
    def _():
        for d in (1, 3, 2):
            arrived(qtraw.at[(y + d) % 4], r_qt.at[d - 1])
        qall[4] = queries(by_rows(qtraw), gq_t)
        for d in (1, 3, 2):
            text_queries(d).start()

    for ch in (1, 2, 4, 3):
        set_keys(ch)
    @pl.when(y == z)
    def _():
        wo_own().wait()

    @pl.when(y != z)
    def _():
        arrived(wo.at[x, y], r_wo.at[y])

    for d in (1, 2, 3):
        arrived(wo.at[x, (y + d) % 4], r_wo.at[(y + d) % 4])

    for d in (1, 3, 2):
        copy_to(wo.at[x], wo.at[x], r_wox.at[d - 1], xpeer(d))

    for d in (1, 3, 2):
        arrived(qall.at[(x + 4 - d) % 4], r_qx.at[d - 1, 0])

    @pl.when(jnp.logical_not(diag))
    def _():
        arrived(qall.at[4], r_qx.at[0, 1])

    r = lax.broadcasted_iota(jnp.int32, (128, 128), 0)
    place = (r // 16) * (4 - 3 * odd) + x * (1 + 3 * odd)
    index = (((r % 16) // 4) * 16 + place) * 4 + r % 4
    usable = (r < 64) & (index < text_len[c])

    def attend(qc, h):
        scores = (
            jnp.dot(kn[h], qall[qc, 128 * h : 128 * h + 128, :], preferred_element_type=F32)
            * FACTOR
        )
        words = jnp.where(usable, scores[512:640], -1e30)
        scores = jnp.concatenate([scores[0:512], words], axis=0)
        highest = jnp.max(scores, axis=0, keepdims=True)
        weights = jnp.exp(scores - highest)
        total = jnp.sum(weights, axis=0, keepdims=True)
        out = jnp.dot(
            vall[128 * h : 128 * h + 128, :], weights.astype(BF16), preferred_element_type=F32
        )
        osend[h, qc] = (out / total).astype(BF16)
        ssend[h, qc, 0:1, :] = highest
        ssend[h, qc, 1:2, :] = total

    ot_first = used[0]
    used[0] += 6
    at_first = used[0]
    used[0] += 9

    def text_out(h, i):
        a, bb = ((osend, otrecv), (ssend, strecv))[i]
        return pltpu.make_async_remote_copy(
            src_ref=a.at[h, 4], dst_ref=bb.at[h, x], send_sem=send.at[ot_first + 2 * h + i],
            recv_sem=r_ot.at[(x + 4 - y) % 4 - 1, h, i], device_id=at_seq(z, y, y),
            device_id_type=MESH,
        )

    def text_att(h, d):
        part = att.at[4, pl.ds(128 * h, 128)]
        return pltpu.make_async_remote_copy(
            src_ref=part, dst_ref=part, send_sem=send.at[at_first + 3 * h + d - 1],
            recv_sem=r_attt.at[h], device_id=ypeer(d), device_id_type=MESH,
        )

    def attend_head(h):
        for d in (2, 1, 3):
            qc = (x + d) % 4
            attend(qc, h)
            copy_to(osend.at[h, qc], orecv.at[h, x], r_o.at[d - 1, h, 0], xpeer(d))
            copy_to(ssend.at[h, qc], srecv.at[h, x], r_o.at[d - 1, h, 1], xpeer(d))
        attend(4, h)

        @pl.when(diag)
        def _():
            otrecv[h, x] = osend[h, 4]
            strecv[h, x] = ssend[h, 4]

        @pl.when(jnp.logical_not(diag))
        def _():
            text_out(h, 0).start()
            text_out(h, 1).start()

        attend(x, h)
        orecv[h, x] = osend[h, x]
        srecv[h, x] = ssend[h, x]

    def combine(o, st, h):
        top = [st[h, i, 0:1, :] for i in range(4)]
        highest = jnp.maximum(jnp.maximum(top[0], top[1]), jnp.maximum(top[2], top[3]))
        share = [st[h, i, 1:2, :] * jnp.exp(top[i] - highest) for i in range(4)]
        total = share[0] + share[1] + share[2] + share[3]
        acc = jnp.zeros((128, 128), F32)
        for i in range(4):
            acc += (share[i] / total) * o[h, i].astype(F32)
        return acc.astype(BF16)

    def combine_head(h):
        part = pl.ds(128 * h, 128)
        for d in (1, 3, 2):
            arrived(orecv.at[h, x], r_o.at[d - 1, h, 0])
            arrived(srecv.at[h, x], r_o.at[d - 1, h, 1])
        att[y, part] = combine(orecv, srecv, h)
        for d in (1, 3, 2):
            copy_to(att.at[y, part], att.at[y, part], r_att.at[d - 1, h], ypeer(d))

        @pl.when(diag)
        def _():
            for d in (1, 3, 2):
                arrived(otrecv.at[h, x], r_ot.at[d - 1, h, 0])
                arrived(strecv.at[h, x], r_ot.at[d - 1, h, 1])
            att[4, part] = combine(otrecv, strecv, h)
            for d in (1, 3, 2):
                text_att(h, d).start()

    attend_head(0)
    attend_head(1)
    combine_head(0)
    attend_head(2)
    combine_head(1)
    combine_head(2)
    for d in (1, 3, 2):
        arrived(wo.at[x], r_wox.at[d - 1])
    weights_out = wo[...].reshape(768, 384)

    def project_out(values, stream):
        out = jnp.dot(weights_out, values, preferred_element_type=F32)
        return natural(
            [
                out[(xx * 4 + yy) * 48 + stream * 24 :][:24]
                for yy in range(4)
                for xx in range(4)
            ]
        ).T

    def video_block(slot):
        block = project_out(att[slot], 0).astype(BF16)
        for q in range(4):
            for j in range(3):
                pout[slot, q, 32 * j : 32 * j + 32, :] = block[
                    32 * q : 32 * q + 32, 128 * j : 128 * j + 128
                ]

    video_block(y)

    @pl.when(jnp.logical_not(diag))
    def _():
        for h in range(3):
            arrived(att.at[4, pl.ds(128 * h, 128)], r_attt.at[h])

    tall[...] = project_out(att[4], 1)
    for yy in range(4):
        for q in range(4):
            for j in range(3):
                pack32[4 * j : 4 * j + 4, 0:128] = tall[
                    16 * yy + 4 * q : 16 * yy + 4 * q + 4, 128 * j : 128 * j + 128
                ]
            tpk[yy, q] = pack32[:, 0:128].astype(BF16)

    own_first = used[0]
    used[0] += 4

    def own_row(dy, slot):
        return pltpu.make_async_remote_copy(
            src_ref=pout.at[slot, y], dst_ref=precv.at[z, y], send_sem=send.at[own_first + dy],
            recv_sem=r_out.at[z, y], device_id=at_seq(slot, y, x), device_id_type=MESH,
        )

    for dy in (0, 1, 3, 2):
        slot = (y + dy) % 4
        if dy:
            for h in range(3):
                arrived(att.at[slot, pl.ds(128 * h, 128)], r_att.at[3 - dy, h])
            video_block(slot)
        for q in range(4):
            pout[slot, q, 96:112, :] = tpk[q, slot]
        for e in (2, 1, 3):
            q = (y + e) % 4
            copy_to(pout.at[slot, q], precv.at[z, y], r_out.at[z, y], at_seq(slot, q, x))

        @pl.when(slot == z)
        def _():
            precv[z, y] = pout[slot, y]

        @pl.when(slot != z)
        def _():
            own_row(dy, slot).start()

    for dy in (0, 1, 3, 2):
        for dz in (0, 1, 3, 2):
            if dy or dz:
                arrived(precv.at[z, y], r_out.at[(z + dz) % 4, (y + dy) % 4])
    for yy in range(4):
        total = precv[0, yy].astype(F32)
        for zz in range(1, 4):
            total += precv[zz, yy].astype(F32)
        total = total.astype(BF16).astype(F32)
        for j in range(3):
            at = pl.ds(384 * yy + 128 * j, 128)
            vout[:, at] = (
                zv[z, :, at].astype(F32) + mod[2:3, at] * total[32 * j : 32 * j + 32]
            ).astype(BF16)
            own = zt[z, 4 * yy : 4 * yy + 4, 128 * j : 128 * j + 128].astype(F32)
            tout[:, at] = (own + mod[5:6, at] * total[96 + 4 * j : 100 + 4 * j]).astype(BF16)

    for op in always:
        op.wait_send()

    for k, d in enumerate(order):
        @pl.when((z + 4 - d) % 4 != y)
        def _():
            query_send(k, (z + 4 - d) % 4).wait_send()

        @pl.when((y + d) % 4 != z)
        def _():
            own_row(d, (y + d) % 4).wait_send()

    @pl.when(y != z)
    def _():
        wo_near().wait_send()

    @pl.when(diag)
    def _():
        for d in (1, 3, 2):
            text_queries(d).wait_send()
            for h in range(3):
                text_att(h, d).wait_send()

    @pl.when(jnp.logical_not(diag))
    def _():
        text_query().wait_send()
        for h in range(3):
            text_out(h, 0).wait_send()
            text_out(h, 1).wait_send()


def body(
    latent_video, text_embed, previous_video, previous_text, noise_blend, modulation,
    w_qkv, w_out, qk_gain, text_len, timestep,
):
    blend = noise_blend.T
    mod = modulation[0].transpose(0, 2, 1, 3)
    gains = qk_gain[0]
    wqkv = w_qkv[0].transpose(0, 1, 3, 2).reshape(144, 1536)
    wout = w_out[0].transpose(0, 2, 1).reshape(48, 1536)
    vm = pl.BlockSpec(memory_space=pltpu.VMEM)
    sm = pl.BlockSpec(memory_space=pltpu.SMEM)
    hbm = pl.BlockSpec(memory_space=pltpu.HBM)

    def buf(*shape, dtype=BF16):
        return pltpu.VMEM(shape, dtype)

    def sems(*shape):
        return pltpu.SemaphoreType.DMA(shape)

    video, words = pl.pallas_call(
        kernel,
        out_shape=(
            jax.ShapeDtypeStruct((32, 1536), BF16),
            jax.ShapeDtypeStruct((4, 1536), BF16),
        ),
        in_specs=[sm, sm] + [hbm] * 9,
        out_specs=(vm, vm),
        scratch_shapes=[
            buf(32, 1536), buf(4, 1536), buf(32, 1536), buf(4, 1536), buf(2, 50, dtype=F32),
            buf(50, 3, 2, 1536, dtype=F32), buf(2, 2, 128, dtype=F32), buf(8, 1536, dtype=F32),
            buf(4, 128, 128, dtype=F32),
            buf(32, 1536), buf(16, 384, dtype=F32), buf(16, 384),
            buf(4, 32, 1536), buf(4, 16, 384), buf(16, 32, 1536), buf(8, 16, 1536),
            buf(4, 144, 1536), buf(2, 288, 1536),
            buf(5, 288, 128), buf(5, 4, 192, 128), buf(4, 96, 128), buf(4, 96, 128),
            buf(5, 384, 128), buf(3, 640, 128), buf(384, 640),
            buf(3, 5, 128, 128), buf(3, 5, 8, 128, dtype=F32),
            buf(3, 4, 128, 128), buf(3, 4, 8, 128, dtype=F32),
            buf(3, 4, 128, 128), buf(3, 4, 8, 128, dtype=F32),
            buf(4, 4, 48, 384), buf(5, 384, 128), buf(128, 384, dtype=F32), buf(4, 4, 16, 128),
            buf(4, 4, 112, 128), buf(4, 4, 112, 128),
            sems(144), sems(4, 2), sems(3, 2), sems(3, 5), sems(4), sems(3), sems(3, 5),
            sems(3, 2), sems(3, 3, 2), sems(3, 3, 2), sems(4), sems(3), sems(3, 3), sems(3),
            sems(4, 4), sems(9),
        ],
        compiler_params=pltpu.CompilerParams(
            collective_id=0, has_side_effects=True, vmem_limit_bytes=48 << 20
        ),
    )(
        timestep, text_len,
        *[
            pltpu.with_memory_space_constraint(a, pltpu.HBM)
            for a in (
                latent_video, text_embed, previous_video[0], previous_text[0],
                blend, mod, gains, wqkv, wout,
            )
        ],
    )
    return video[None], words[None]


def solution(mesh):
    placed = (
        P("seq", None),
        P("seq", None),
        P("comp", "seq", None),
        P("comp", "seq", None),
        P(),
        P("comp", None, None, None, None),
        P("comp", None, None, None, "seq"),
        P("comp", None, None, "seq"),
        P("comp", None, None, None),
        P(),
        P(),
    )
    return jax.shard_map(
        body,
        mesh=mesh,
        in_specs=placed,
        out_specs=(P("comp", "seq", None), P("comp", "seq", None)),
        check_vma=False,
    )
```

```python
import math

import jax
import jax.numpy as jnp
from jax import lax
from jax.experimental import pallas as pl
from jax.experimental.pallas import tpu as pltpu
from jax.sharding import PartitionSpec as P

HEAD_DIM = 128
F32, BF16 = jnp.float32, jnp.bfloat16
MESH = pl.DeviceIdType.MESH
FACTOR = 1.0 / math.sqrt(HEAD_DIM)


def kernel(
    timestep, text_len, latent, text, prev_v, prev_t, blend_hbm, mod_hbm, gains_hbm, wqkv, wout,
    vout, tout,
    latent_v, text_v, old_v, old_t, blend, mod_all, gains, mod, turned,
    vsend, pack32, tsend, zv, zt, tokv, tokt, wq, packed,
    b, kv, qraw, qtraw, qall, kn, vall,
    osend, ssend, orecv, srecv, otrecv, strecv,
    wo, att, tall, own_words, pout, precv,
    send, r_z, r_w, r_y, r_q, r_qt, r_kv, r_qx, r_o, r_ot,
    r_wo, r_wox, r_att, r_attt, r_out, loc,
):
    c = lax.axis_index("comp")
    s = lax.axis_index("seq")
    odd = c % 2
    z, a0, a1 = s // 16, (s // 4) % 4, s % 4
    y = a0 + odd * (a1 - a0)
    x = a1 + odd * (a0 - a1)
    diag = y == x

    def at_seq(zz, yy, xx):
        return (c, zz * 16 + yy * (4 - 3 * odd) + xx * (1 + 3 * odd))

    def ypeer(d):
        return at_seq(z, (y + d) % 4, x)

    def zypeer(dz, dy):
        return at_seq((z + dz) % 4, (y + dy) % 4, x)

    def xpeer(d):
        return at_seq(z, y, (x + d) % 4)

    used = [0]
    always, on_diag, off_diag = [], [], []

    def copy_to(src, dst, recv, device, group=None):
        op = pltpu.make_async_remote_copy(
            src_ref=src, dst_ref=dst, send_sem=send.at[used[0]], recv_sem=recv,
            device_id=device, device_id_type=MESH,
        )
        used[0] += 1
        op.start()
        (always if group is None else group).append(op)

    def arrived(dst, recv):
        pltpu.make_async_remote_copy(
            src_ref=dst, dst_ref=dst, send_sem=send.at[0], recv_sem=recv,
            device_id=xpeer(1), device_id_type=MESH,
        ).wait_recv()

    nextc, prevc = (c + 1) % 4, (c + 3) % 4
    barrier = pltpu.get_barrier_semaphore()
    for d in range(4):
        pl.semaphore_signal(barrier, inc=1, device_id=(prevc, (s + 16 * d) % 64), device_id_type=MESH)
    for dz in range(4):
        for dy in range(4):
            if dz or dy:
                pl.semaphore_signal(barrier, inc=1, device_id=zypeer(dz, dy), device_id_type=MESH)
    for d in (1, 2, 3):
        pl.semaphore_signal(barrier, inc=1, device_id=xpeer(d), device_id_type=MESH)

    loads = [
        pltpu.make_async_copy(a, bb, loc.at[i])
        for i, (a, bb) in enumerate(
            (
                (latent, latent_v), (prev_v, old_v), (text, text_v), (prev_t, old_t),
                (blend_hbm, blend), (mod_hbm, mod_all), (gains_hbm, gains), (wqkv, wq.at[x]),
            )
        )
    ]
    for op in loads:
        op.start()
    for op in loads[:5]:
        op.wait()

    step = timestep[0]
    lane = lax.broadcasted_iota(jnp.int32, (2, 50), 1)
    pair = jnp.sum(jnp.where(lane == step, blend[...], 0.0), axis=1, keepdims=True)
    last = c == 3
    old = old_v[...]
    mixed = (pair[0:1] * latent_v[...].astype(F32) + pair[1:2] * old.astype(F32)).astype(BF16)
    vsend[...] = jnp.where(last, mixed, old)
    words = jnp.where(last, text_v[...], old_t[...]).astype(F32)
    for j in range(4):
        pack32[4 * j : 4 * j + 4, :] = words[:, 384 * j : 384 * j + 384]
    tsend[...] = pack32[...].astype(BF16)
    tokt[4:8] = jnp.zeros((4, 16, 1536), BF16)
    pl.semaphore_wait(barrier, 22)

    for d in (2, 1, 3, 0):
        copy_to(tsend, zt.at[z], r_z.at[d, 1], (nextc, (s + 16 * d) % 64))
    for d in (0, 1, 3, 2):
        copy_to(vsend, zv.at[z], r_z.at[d, 0], (nextc, (s + 16 * d) % 64))
    for i, part in enumerate((pl.ds(0, 80), pl.ds(80, 64))):
        for d in (1, 3, 2):
            copy_to(wqkv.at[part], wq.at[x, part], r_w.at[d - 1, i], xpeer(d))

    for op in loads[5:7]:
        op.wait()
    for st in range(2):
        for k in range(3):
            mod[3 * st + k : 3 * st + k + 1, :] = mod_all[step, k, st : st + 1, :]
        for k in range(2):
            turned[2 * st + k] = jnp.broadcast_to(gains[st, k : k + 1, :], (128, 128)).T

    def normed(wide, stream):
        center = wide - jnp.mean(wide, axis=-1, keepdims=True)
        spread = jnp.mean(center * center, axis=-1, keepdims=True)
        shift = mod[3 * stream : 3 * stream + 1, :]
        scale = mod[3 * stream + 1 : 3 * stream + 2, :]
        return (center * lax.rsqrt(spread + 1e-06) * (1.0 + scale) + shift).astype(BF16)

    def unpack(packed):
        return jnp.concatenate([packed[4 * j : 4 * j + 4, :] for j in range(4)], axis=1)

    def norm_piece(d):
        zz = (z + 4 - d) % 4
        arrived(zv.at[zz], r_z.at[d, 0])
        slot = zz * 4 + y
        tokv[slot] = normed(zv[zz].astype(F32), 0)
        for e in (1, 3, 2):
            copy_to(tokv.at[slot], tokv.at[slot], r_y.at[e - 1, d], ypeer(e))

    norm_piece(0)
    for d in (0, 1, 3, 2):
        arrived(zt.at[(z + 4 - d) % 4], r_z.at[d, 1])
    rows = jnp.concatenate([unpack(zt[j].astype(F32)) for j in range(4)], axis=0)
    tokt[y] = normed(rows, 1)
    for e in (1, 3, 2):
        copy_to(tokt.at[y], tokt.at[y], r_y.at[e - 1, 4], ypeer(e))
    norm_piece(1)
    norm_piece(3)

    loads[7].wait()

    def regroup(stream):
        wide = [wq[xx, 72 * stream : 72 * stream + 72].astype(F32) for xx in range(4)]
        packed[stream] = jnp.concatenate(
            [wide[xx][24 * j : 24 * j + 24] for j in range(3) for xx in range(4)], axis=0
        ).astype(BF16)

    def project(tokens, stream):
        return lax.dot_general(
            packed[stream], tokens, (((1,), (1,)), ((), ())), preferred_element_type=F32
        ).astype(BF16)

    def natural(groups):
        straight = [groups[g] for g in range(16)]
        crossed = [groups[(g % 4) * 4 + g // 4] for g in range(16)]
        return jnp.where(
            odd == 1, jnp.concatenate(crossed, axis=0), jnp.concatenate(straight, axis=0)
        )

    def by_rows(slabs):
        wide = [slabs[yy].astype(F32) for yy in range(4)]
        return natural([wide[g // 4][24 * (g % 4) : 24 * (g % 4) + 24] for g in range(16)])

    def head_norm(raw, gain):
        square = jnp.mean(raw * raw, axis=0, keepdims=True)
        return raw * lax.rsqrt(square + 1e-06) * gain

    gq_v, gk_v, gq_t, gk_t = [turned[j] for j in range(4)]

    def queries(raw, gain):
        return jnp.concatenate(
            [head_norm(raw[128 * h : 128 * h + 128], gain) for h in range(3)], axis=0
        ).astype(BF16)

    def set_keys(ch):
        for e in (1, 3, 2):
            arrived(kv.at[ch, 0], r_kv.at[e - 1, ch])
        keys = by_rows([kv[ch, yy, 0:96] for yy in range(4)])
        values = by_rows([kv[ch, yy, 96:192] for yy in range(4)])
        vall[:, 128 * ch : 128 * ch + 128] = values.astype(BF16)
        for h in range(3):
            key = head_norm(keys[128 * h : 128 * h + 128], gk_v if ch < 4 else gk_t)
            kn[h, 128 * ch : 128 * ch + 128, :] = key.astype(BF16).T

    query_first = used[0]
    used[0] += 4

    def query_send(k, zz):
        return pltpu.make_async_remote_copy(
            src_ref=b.at[k, 0:96], dst_ref=qraw.at[y], send_sem=send.at[query_first + k],
            recv_sem=r_q.at[y], device_id=at_seq(z, zz, x), device_id_type=MESH,
        )

    order = (0, 1, 3, 2)

    def video_chunk(k):
        d = order[k]
        zz = (z + 4 - d) % 4
        for e in (1, 3, 2):
            arrived(tokv.at[zz * 4 + (y + 4 - e) % 4], r_y.at[e - 1, d])
        b[k] = project(tokv[pl.ds(zz * 4, 4)].reshape(128, 1536), 0)

        @pl.when(zz == y)
        def _():
            qraw[y] = b[k, 0:96]

        @pl.when(zz != y)
        def _():
            query_send(k, zz).start()

        for e in (1, 3, 2):
            copy_to(b.at[k, 96:288], kv.at[k, y], r_kv.at[e - 1, k], ypeer(e))
        kv[k, y] = b[k, 96:288]

    for d in (1, 3, 2):
        arrived(wq.at[(x + 4 - d) % 4, pl.ds(0, 80)], r_w.at[d - 1, 0])
    regroup(0)
    video_chunk(0)
    norm_piece(2)
    def wo_part(d):
        return wout.at[:, pl.ds(pl.multiple_of(((z + d) % 4) * 384, 128), 384)]

    for d in (1, 3, 2):
        copy_to(wo_part(d), wo.at[x, y], r_wo.at[y], at_seq((z + d) % 4, z, x))
    wo_slot = used[0]
    used[0] += 1

    def wo_near():
        return pltpu.make_async_remote_copy(
            src_ref=wo_part(0), dst_ref=wo.at[x, y], send_sem=send.at[wo_slot],
            recv_sem=r_wo.at[y], device_id=at_seq(z, z, x), device_id_type=MESH,
        )

    def wo_own():
        return pltpu.make_async_copy(wo_part(0), wo.at[x, y], loc.at[8])

    @pl.when(y == z)
    def _():
        wo_own().start()

    @pl.when(y != z)
    def _():
        wo_near().start()

    video_chunk(1)
    video_chunk(2)
    for d in (1, 3, 2):
        arrived(wq.at[(x + 4 - d) % 4, pl.ds(80, 64)], r_w.at[d - 1, 1])
    regroup(1)
    for e in (1, 3, 2):
        arrived(tokt.at[(y + 4 - e) % 4], r_y.at[e - 1, 4])
    b[4] = project(tokt[...].reshape(128, 1536), 1)
    to_diag = (y + 4 - x) % 4
    used_qt = used[0]
    used[0] += 1

    def text_query():
        return pltpu.make_async_remote_copy(
            src_ref=b.at[4, 0:96], dst_ref=qtraw.at[y], send_sem=send.at[used_qt],
            recv_sem=r_qt.at[to_diag - 1], device_id=at_seq(z, x, x), device_id_type=MESH,
        )

    @pl.when(diag)
    def _():
        qtraw[y] = b[4, 0:96]

    @pl.when(jnp.logical_not(diag))
    def _():
        text_query().start()

    for e in (1, 3, 2):
        copy_to(b.at[4, 96:288], kv.at[4, y], r_kv.at[e - 1, 4], ypeer(e))
    kv[4, y] = b[4, 96:288]

    set_keys(0)
    video_chunk(3)
    for d in (1, 3, 2):
        arrived(qraw.at[(y + d) % 4], r_q.at[(y + d) % 4])
    qall[x] = queries(by_rows(qraw), gq_v)
    for d in (1, 3, 2):
        copy_to(qall.at[x], qall.at[x], r_qx.at[d - 1, 0], xpeer(d))
    qt_first = used[0]
    used[0] += 3

    def text_queries(d):
        return pltpu.make_async_remote_copy(
            src_ref=qall.at[4], dst_ref=qall.at[4], send_sem=send.at[qt_first + d - 1],
            recv_sem=r_qx.at[0, 1], device_id=xpeer(d), device_id_type=MESH,
        )

    @pl.when(diag)
    def _():
        for d in (1, 3, 2):
            arrived(qtraw.at[(y + d) % 4], r_qt.at[d - 1])
        qall[4] = queries(by_rows(qtraw), gq_t)
        for d in (1, 3, 2):
            text_queries(d).start()

    for ch in (1, 2, 4, 3):
        set_keys(ch)
    @pl.when(y == z)
    def _():
        wo_own().wait()

    @pl.when(y != z)
    def _():
        arrived(wo.at[x, y], r_wo.at[y])

    for d in (1, 2, 3):
        arrived(wo.at[x, (y + d) % 4], r_wo.at[(y + d) % 4])

    for d in (1, 3, 2):
        copy_to(wo.at[x], wo.at[x], r_wox.at[d - 1], xpeer(d))

    for d in (1, 3, 2):
        arrived(qall.at[(x + 4 - d) % 4], r_qx.at[d - 1, 0])

    @pl.when(jnp.logical_not(diag))
    def _():
        arrived(qall.at[4], r_qx.at[0, 1])

    r = lax.broadcasted_iota(jnp.int32, (128, 256), 0)
    place = (r // 16) * (4 - 3 * odd) + x * (1 + 3 * odd)
    index = (((r % 16) // 4) * 16 + place) * 4 + r % 4
    usable = (r < 64) & (index < text_len[c])

    def attend(slots, h):
        wide = 128 * len(slots)
        queries_in = jnp.concatenate(
            [qall[slot, 128 * h : 128 * h + 128, :] for slot in slots], axis=1
        )
        scores = jnp.dot(kn[h], queries_in, preferred_element_type=F32) * FACTOR
        words = jnp.where(usable[:, 0:wide], scores[512:640], -1e30)
        scores = jnp.concatenate([scores[0:512], words], axis=0)
        highest = jnp.max(scores, axis=0, keepdims=True)
        weights = jnp.exp(scores - highest)
        total = jnp.sum(weights, axis=0, keepdims=True)
        out = jnp.dot(
            vall[128 * h : 128 * h + 128, :], weights.astype(BF16), preferred_element_type=F32
        )
        out = (out / total).astype(BF16)
        for i, slot in enumerate(slots):
            part = slice(128 * i, 128 * i + 128)
            osend[h, slot] = out[:, part]
            ssend[h, slot, 0:1, :] = highest[:, part]
            ssend[h, slot, 1:2, :] = total[:, part]

    ot_first = used[0]
    used[0] += 6
    at_first = used[0]
    used[0] += 9

    def text_out(h, i):
        a, bb = ((osend, otrecv), (ssend, strecv))[i]
        return pltpu.make_async_remote_copy(
            src_ref=a.at[h, 4], dst_ref=bb.at[h, x], send_sem=send.at[ot_first + 2 * h + i],
            recv_sem=r_ot.at[(x + 4 - y) % 4 - 1, h, i], device_id=at_seq(z, y, y),
            device_id_type=MESH,
        )

    def text_att(h, d):
        part = att.at[4, pl.ds(128 * h, 128)]
        return pltpu.make_async_remote_copy(
            src_ref=part, dst_ref=part, send_sem=send.at[at_first + 3 * h + d - 1],
            recv_sem=r_attt.at[h], device_id=ypeer(d), device_id_type=MESH,
        )

    def attend_head(h):
        def send_part(d):
            qc = (x + d) % 4
            copy_to(osend.at[h, qc], orecv.at[h, x], r_o.at[d - 1, h, 0], xpeer(d))
            copy_to(ssend.at[h, qc], srecv.at[h, x], r_o.at[d - 1, h, 1], xpeer(d))

        attend(((x + 2) % 4, (x + 1) % 4), h)
        send_part(2)
        send_part(1)
        attend(((x + 3) % 4, 4), h)
        send_part(3)

        @pl.when(diag)
        def _():
            otrecv[h, x] = osend[h, 4]
            strecv[h, x] = ssend[h, 4]

        @pl.when(jnp.logical_not(diag))
        def _():
            text_out(h, 0).start()
            text_out(h, 1).start()

        attend((x,), h)
        orecv[h, x] = osend[h, x]
        srecv[h, x] = ssend[h, x]

    def combine(o, st, h):
        top = [st[h, i, 0:1, :] for i in range(4)]
        highest = jnp.maximum(jnp.maximum(top[0], top[1]), jnp.maximum(top[2], top[3]))
        share = [st[h, i, 1:2, :] * jnp.exp(top[i] - highest) for i in range(4)]
        total = share[0] + share[1] + share[2] + share[3]
        acc = jnp.zeros((128, 128), F32)
        for i in range(4):
            acc += (share[i] / total) * o[h, i].astype(F32)
        return acc.astype(BF16)

    def combine_head(h):
        part = pl.ds(128 * h, 128)
        for d in (1, 3, 2):
            arrived(orecv.at[h, x], r_o.at[d - 1, h, 0])
            arrived(srecv.at[h, x], r_o.at[d - 1, h, 1])
        att[y, part] = combine(orecv, srecv, h)
        for d in (1, 3, 2):
            copy_to(att.at[y, part], att.at[y, part], r_att.at[d - 1, h], ypeer(d))

        @pl.when(diag)
        def _():
            for d in (1, 3, 2):
                arrived(otrecv.at[h, x], r_ot.at[d - 1, h, 0])
                arrived(strecv.at[h, x], r_ot.at[d - 1, h, 1])
            att[4, part] = combine(otrecv, strecv, h)
            for d in (1, 3, 2):
                text_att(h, d).start()

    attend_head(0)
    attend_head(1)
    combine_head(0)
    attend_head(2)
    combine_head(1)
    combine_head(2)
    for d in (1, 3, 2):
        arrived(wo.at[x], r_wox.at[d - 1])
    weights_out = wo[...].reshape(768, 384)

    def project_out(values, stream):
        out = jnp.dot(weights_out, values, preferred_element_type=F32)
        return natural(
            [
                out[(xx * 4 + yy) * 48 + stream * 24 :][:24]
                for yy in range(4)
                for xx in range(4)
            ]
        ).T

    def video_block(slot):
        block = project_out(att[slot], 0).astype(BF16)
        for q in range(4):
            for j in range(3):
                pout[slot, q, 32 * j : 32 * j + 32, :] = block[
                    32 * q : 32 * q + 32, 128 * j : 128 * j + 128
                ]

    video_block(y)

    own_first = used[0]
    used[0] += 8
    rows_of = (pl.ds(0, 96), pl.ds(96, 16))

    def own_row(dy, i):
        slot = (y + dy) % 4
        return pltpu.make_async_remote_copy(
            src_ref=pout.at[slot, y, rows_of[i]], dst_ref=precv.at[z, y, rows_of[i]],
            send_sem=send.at[own_first + 2 * dy + i], recv_sem=r_out.at[z, y, i],
            device_id=at_seq(slot, y, x), device_id_type=MESH,
        )

    def leave(dy, i):
        slot = (y + dy) % 4
        for e in (2, 1, 3):
            q = (y + e) % 4
            copy_to(
                pout.at[slot, q, rows_of[i]], precv.at[z, y, rows_of[i]], r_out.at[z, y, i],
                at_seq(slot, q, x),
            )

        @pl.when(slot == z)
        def _():
            precv[z, y, rows_of[i], :] = pout[slot, y, rows_of[i], :]

        @pl.when(slot != z)
        def _():
            own_row(dy, i).start()

    own_words[...] = unpack(zt[z].astype(F32))
    leave(0, 0)
    for dy in (1, 3, 2):
        slot = (y + dy) % 4
        for h in range(3):
            arrived(att.at[slot, pl.ds(128 * h, 128)], r_att.at[3 - dy, h])
        video_block(slot)
        leave(dy, 0)

    @pl.when(jnp.logical_not(diag))
    def _():
        for h in range(3):
            arrived(att.at[4, pl.ds(128 * h, 128)], r_attt.at[h])

    tall[...] = project_out(att[4], 1)
    for yy in range(4):
        for q in range(4):
            for j in range(3):
                pack32[4 * j : 4 * j + 4, 0:128] = tall[
                    16 * yy + 4 * q : 16 * yy + 4 * q + 4, 128 * j : 128 * j + 128
                ]
            pout[q, yy, 96:112, :] = pack32[:, 0:128].astype(BF16)

    for dy in (0, 1, 3, 2):
        leave(dy, 1)

    for dy in (0, 1, 3, 2):
        yy = (y + dy) % 4
        for dz in (0, 1, 3, 2):
            if dy or dz:
                for i in range(2):
                    arrived(precv.at[z, y, rows_of[i]], r_out.at[(z + dz) % 4, yy, i])
        total = precv[0, yy].astype(F32)
        for zz in range(1, 4):
            total += precv[zz, yy].astype(F32)
        total = total.astype(BF16).astype(F32)
        for j in range(3):
            at = pl.ds(pl.multiple_of(384 * yy + 128 * j, 128), 128)
            vout[:, at] = (
                zv[z, :, at].astype(F32) + mod[2:3, at] * total[32 * j : 32 * j + 32]
            ).astype(BF16)
            own = own_words[:, at]
            tout[:, at] = (own + mod[5:6, at] * total[96 + 4 * j : 100 + 4 * j]).astype(BF16)

    for op in always:
        op.wait_send()

    for k, d in enumerate(order):
        @pl.when((z + 4 - d) % 4 != y)
        def _():
            query_send(k, (z + 4 - d) % 4).wait_send()

        @pl.when((y + d) % 4 != z)
        def _():
            for i in range(2):
                own_row(d, i).wait_send()

    @pl.when(y != z)
    def _():
        wo_near().wait_send()

    @pl.when(diag)
    def _():
        for d in (1, 3, 2):
            text_queries(d).wait_send()
            for h in range(3):
                text_att(h, d).wait_send()

    @pl.when(jnp.logical_not(diag))
    def _():
        text_query().wait_send()
        for h in range(3):
            text_out(h, 0).wait_send()
            text_out(h, 1).wait_send()


def body(
    latent_video, text_embed, previous_video, previous_text, noise_blend, modulation,
    w_qkv, w_out, qk_gain, text_len, timestep,
):
    blend = noise_blend.T
    mod = modulation[0].transpose(0, 2, 1, 3)
    gains = qk_gain[0]
    wqkv = w_qkv[0].transpose(0, 1, 3, 2).reshape(144, 1536)
    wout = w_out[0].transpose(0, 2, 1).reshape(48, 1536)
    vm = pl.BlockSpec(memory_space=pltpu.VMEM)
    sm = pl.BlockSpec(memory_space=pltpu.SMEM)
    hbm = pl.BlockSpec(memory_space=pltpu.HBM)

    def buf(*shape, dtype=BF16):
        return pltpu.VMEM(shape, dtype)

    def sems(*shape):
        return pltpu.SemaphoreType.DMA(shape)

    video, words = pl.pallas_call(
        kernel,
        out_shape=(
            jax.ShapeDtypeStruct((32, 1536), BF16),
            jax.ShapeDtypeStruct((4, 1536), BF16),
        ),
        in_specs=[sm, sm] + [hbm] * 9,
        out_specs=(vm, vm),
        scratch_shapes=[
            buf(32, 1536), buf(4, 1536), buf(32, 1536), buf(4, 1536), buf(2, 50, dtype=F32),
            buf(50, 3, 2, 1536, dtype=F32), buf(2, 2, 128, dtype=F32), buf(8, 1536, dtype=F32),
            buf(4, 128, 128, dtype=F32),
            buf(32, 1536), buf(16, 384, dtype=F32), buf(16, 384),
            buf(4, 32, 1536), buf(4, 16, 384), buf(16, 32, 1536), buf(8, 16, 1536),
            buf(4, 144, 1536), buf(2, 288, 1536),
            buf(5, 288, 128), buf(5, 4, 192, 128), buf(4, 96, 128), buf(4, 96, 128),
            buf(5, 384, 128), buf(3, 640, 128), buf(384, 640),
            buf(3, 5, 128, 128), buf(3, 5, 8, 128, dtype=F32),
            buf(3, 4, 128, 128), buf(3, 4, 8, 128, dtype=F32),
            buf(3, 4, 128, 128), buf(3, 4, 8, 128, dtype=F32),
            buf(4, 4, 48, 384), buf(5, 384, 128), buf(128, 384, dtype=F32), buf(4, 1536, dtype=F32),
            buf(4, 4, 112, 128), buf(4, 4, 112, 128),
            sems(176), sems(4, 2), sems(3, 2), sems(3, 5), sems(4), sems(3), sems(3, 5),
            sems(3, 2), sems(3, 3, 2), sems(3, 3, 2), sems(4), sems(3), sems(3, 3), sems(3),
            sems(4, 4, 2), sems(9),
        ],
        compiler_params=pltpu.CompilerParams(
            collective_id=0, has_side_effects=True, vmem_limit_bytes=48 << 20
        ),
    )(
        timestep, text_len,
        *[
            pltpu.with_memory_space_constraint(a, pltpu.HBM)
            for a in (
                latent_video, text_embed, previous_video[0], previous_text[0],
                blend, mod, gains, wqkv, wout,
            )
        ],
    )
    return video[None], words[None]


def solution(mesh):
    placed = (
        P("seq", None),
        P("seq", None),
        P("comp", "seq", None),
        P("comp", "seq", None),
        P(),
        P("comp", None, None, None, None),
        P("comp", None, None, None, "seq"),
        P("comp", None, None, "seq"),
        P("comp", None, None, None),
        P(),
        P(),
    )
    return jax.shard_map(
        body,
        mesh=mesh,
        in_specs=placed,
        out_specs=(P("comp", "seq", None), P("comp", "seq", None)),
        check_vma=False,
    )
```

```python
import math

import jax
import jax.numpy as jnp
from jax import lax
from jax.experimental import pallas as pl
from jax.experimental.pallas import tpu as pltpu
from jax.sharding import PartitionSpec as P

HEAD_DIM = 128
F32, BF16 = jnp.float32, jnp.bfloat16
MESH = pl.DeviceIdType.MESH
FACTOR = 1.0 / math.sqrt(HEAD_DIM)


def kernel(
    timestep, text_len, latent, text, prev_v, prev_t, blend_hbm, mod_hbm, gains_hbm, wqkv, wout,
    vout, tout,
    latent_v, text_v, old_v, old_t, blend, mod_all, gains, mod, turned,
    vsend, pack32, tsend, zv, zt, tokv, tokt, wq, packed,
    b, kv, qraw, qtraw, qall, kn, vall,
    osend, ssend, orecv, srecv, otrecv, strecv,
    wo, att, tall, own_words, pout, precv,
    send, r_z, r_w, r_y, r_q, r_qt, r_kv, r_qx, r_o, r_ot,
    r_wo, r_wox, r_att, r_attt, r_out, loc,
):
    c = lax.axis_index("comp")
    s = lax.axis_index("seq")
    odd = c % 2
    z, a0, a1 = s // 16, (s // 4) % 4, s % 4
    y = a0 + odd * (a1 - a0)
    x = a1 + odd * (a0 - a1)
    diag = y == x

    def at_seq(zz, yy, xx):
        return (c, zz * 16 + yy * (4 - 3 * odd) + xx * (1 + 3 * odd))

    def ypeer(d):
        return at_seq(z, (y + d) % 4, x)

    def zypeer(dz, dy):
        return at_seq((z + dz) % 4, (y + dy) % 4, x)

    def xpeer(d):
        return at_seq(z, y, (x + d) % 4)

    used = [0]
    always, on_diag, off_diag = [], [], []

    def copy_to(src, dst, recv, device, group=None):
        op = pltpu.make_async_remote_copy(
            src_ref=src, dst_ref=dst, send_sem=send.at[used[0]], recv_sem=recv,
            device_id=device, device_id_type=MESH,
        )
        used[0] += 1
        op.start()
        (always if group is None else group).append(op)

    def arrived(dst, recv):
        pltpu.make_async_remote_copy(
            src_ref=dst, dst_ref=dst, send_sem=send.at[0], recv_sem=recv,
            device_id=xpeer(1), device_id_type=MESH,
        ).wait_recv()

    nextc, prevc = (c + 1) % 4, (c + 3) % 4
    barrier = pltpu.get_barrier_semaphore()
    for d in range(4):
        pl.semaphore_signal(barrier, inc=1, device_id=(prevc, (s + 16 * d) % 64), device_id_type=MESH)
    for dz in range(4):
        for dy in range(4):
            if dz or dy:
                pl.semaphore_signal(barrier, inc=1, device_id=zypeer(dz, dy), device_id_type=MESH)
    for d in (1, 2, 3):
        pl.semaphore_signal(barrier, inc=1, device_id=xpeer(d), device_id_type=MESH)

    loads = [
        pltpu.make_async_copy(a, bb, loc.at[i])
        for i, (a, bb) in enumerate(
            (
                (latent, latent_v), (prev_v, old_v), (text, text_v), (prev_t, old_t),
                (blend_hbm, blend), (mod_hbm, mod_all), (gains_hbm, gains), (wqkv, wq.at[x]),
            )
        )
    ]
    for op in loads:
        op.start()
    for op in loads[:5]:
        op.wait()

    step = timestep[0]
    lane = lax.broadcasted_iota(jnp.int32, (2, 50), 1)
    pair = jnp.sum(jnp.where(lane == step, blend[...], 0.0), axis=1, keepdims=True)
    last = c == 3
    old = old_v[...]
    mixed = (pair[0:1] * latent_v[...].astype(F32) + pair[1:2] * old.astype(F32)).astype(BF16)
    vsend[...] = jnp.where(last, mixed, old)
    words = jnp.where(last, text_v[...], old_t[...]).astype(F32)
    for j in range(4):
        pack32[4 * j : 4 * j + 4, :] = words[:, 384 * j : 384 * j + 384]
    tsend[...] = pack32[...].astype(BF16)
    tokt[4:8] = jnp.zeros((4, 16, 1536), BF16)
    pl.semaphore_wait(barrier, 22)

    for d in (2, 1, 3, 0):
        copy_to(tsend, zt.at[z], r_z.at[d, 1], (nextc, (s + 16 * d) % 64))
    for d in (0, 1, 3, 2):
        copy_to(vsend, zv.at[z], r_z.at[d, 0], (nextc, (s + 16 * d) % 64))
    for i, part in enumerate((pl.ds(0, 80), pl.ds(80, 64))):
        for d in (1, 3, 2):
            copy_to(wqkv.at[part], wq.at[x, part], r_w.at[d - 1, i], xpeer(d))

    for op in loads[5:7]:
        op.wait()
    for st in range(2):
        for k in range(3):
            mod[3 * st + k : 3 * st + k + 1, :] = mod_all[step, k, st : st + 1, :]
        for k in range(2):
            turned[2 * st + k] = jnp.broadcast_to(gains[st, k : k + 1, :], (128, 128)).T

    def normed(wide, stream):
        center = wide - jnp.mean(wide, axis=-1, keepdims=True)
        spread = jnp.mean(center * center, axis=-1, keepdims=True)
        shift = mod[3 * stream : 3 * stream + 1, :]
        scale = mod[3 * stream + 1 : 3 * stream + 2, :]
        return (center * lax.rsqrt(spread + 1e-06) * (1.0 + scale) + shift).astype(BF16)

    def unpack(packed):
        return jnp.concatenate([packed[4 * j : 4 * j + 4, :] for j in range(4)], axis=1)

    def norm_piece(d):
        zz = (z + 4 - d) % 4
        arrived(zv.at[zz], r_z.at[d, 0])
        slot = zz * 4 + y
        tokv[slot] = normed(zv[zz].astype(F32), 0)
        for e in (2, 1, 3):
            copy_to(tokv.at[slot], tokv.at[slot], r_y.at[e - 1, d], ypeer(e))

    norm_piece(0)
    for d in (0, 1, 3, 2):
        arrived(zt.at[(z + 4 - d) % 4], r_z.at[d, 1])
    rows = jnp.concatenate([unpack(zt[j].astype(F32)) for j in range(4)], axis=0)
    tokt[y] = normed(rows, 1)
    for e in (2, 1, 3):
        copy_to(tokt.at[y], tokt.at[y], r_y.at[e - 1, 4], ypeer(e))
    norm_piece(1)
    norm_piece(3)

    loads[7].wait()

    def regroup(stream):
        wide = [wq[xx, 72 * stream : 72 * stream + 72].astype(F32) for xx in range(4)]
        packed[stream] = jnp.concatenate(
            [wide[xx][24 * j : 24 * j + 24] for j in range(3) for xx in range(4)], axis=0
        ).astype(BF16)

    def project(tokens, stream):
        return lax.dot_general(
            packed[stream], tokens, (((1,), (1,)), ((), ())), preferred_element_type=F32
        ).astype(BF16)

    def natural(groups):
        straight = [groups[g] for g in range(16)]
        crossed = [groups[(g % 4) * 4 + g // 4] for g in range(16)]
        return jnp.where(
            odd == 1, jnp.concatenate(crossed, axis=0), jnp.concatenate(straight, axis=0)
        )

    def by_rows(slabs):
        wide = [slabs[yy].astype(F32) for yy in range(4)]
        return natural([wide[g // 4][24 * (g % 4) : 24 * (g % 4) + 24] for g in range(16)])

    def head_norm(raw, gain):
        square = jnp.mean(raw * raw, axis=0, keepdims=True)
        return raw * lax.rsqrt(square + 1e-06) * gain

    gq_v, gk_v, gq_t, gk_t = [turned[j] for j in range(4)]

    def queries(raw, gain):
        return jnp.concatenate(
            [head_norm(raw[128 * h : 128 * h + 128], gain) for h in range(3)], axis=0
        ).astype(BF16)

    def set_keys(ch):
        for e in (2, 1, 3):
            arrived(kv.at[ch, 0], r_kv.at[e - 1, ch])
        keys = by_rows([kv[ch, yy, 0:96] for yy in range(4)])
        values = by_rows([kv[ch, yy, 96:192] for yy in range(4)])
        vall[:, 128 * ch : 128 * ch + 128] = values.astype(BF16)
        for h in range(3):
            key = head_norm(keys[128 * h : 128 * h + 128], gk_v if ch < 4 else gk_t)
            kn[h, 128 * ch : 128 * ch + 128, :] = key.astype(BF16).T

    query_first = used[0]
    used[0] += 4

    def query_send(k, zz):
        return pltpu.make_async_remote_copy(
            src_ref=b.at[k, 0:96], dst_ref=qraw.at[y], send_sem=send.at[query_first + k],
            recv_sem=r_q.at[y], device_id=at_seq(z, zz, x), device_id_type=MESH,
        )

    order = (0, 1, 3, 2)

    def video_chunk(k):
        d = order[k]
        zz = (z + 4 - d) % 4
        for e in (2, 1, 3):
            arrived(tokv.at[zz * 4 + (y + 4 - e) % 4], r_y.at[e - 1, d])
        b[k] = project(tokv[pl.ds(zz * 4, 4)].reshape(128, 1536), 0)

        @pl.when(zz == y)
        def _():
            qraw[y] = b[k, 0:96]

        @pl.when(zz != y)
        def _():
            query_send(k, zz).start()

        for e in (2, 1, 3):
            copy_to(b.at[k, 96:288], kv.at[k, y], r_kv.at[e - 1, k], ypeer(e))
        kv[k, y] = b[k, 96:288]

    for d in (1, 3, 2):
        arrived(wq.at[(x + 4 - d) % 4, pl.ds(0, 80)], r_w.at[d - 1, 0])
    regroup(0)
    video_chunk(0)
    norm_piece(2)
    def wo_part(d):
        return wout.at[:, pl.ds(pl.multiple_of(((z + d) % 4) * 384, 128), 384)]

    for d in (1, 3, 2):
        copy_to(wo_part(d), wo.at[x, y], r_wo.at[y], at_seq((z + d) % 4, z, x))
    wo_slot = used[0]
    used[0] += 1

    def wo_near():
        return pltpu.make_async_remote_copy(
            src_ref=wo_part(0), dst_ref=wo.at[x, y], send_sem=send.at[wo_slot],
            recv_sem=r_wo.at[y], device_id=at_seq(z, z, x), device_id_type=MESH,
        )

    def wo_own():
        return pltpu.make_async_copy(wo_part(0), wo.at[x, y], loc.at[8])

    @pl.when(y == z)
    def _():
        wo_own().start()

    @pl.when(y != z)
    def _():
        wo_near().start()

    video_chunk(1)
    video_chunk(2)
    for d in (1, 3, 2):
        arrived(wq.at[(x + 4 - d) % 4, pl.ds(80, 64)], r_w.at[d - 1, 1])
    regroup(1)
    for e in (2, 1, 3):
        arrived(tokt.at[(y + 4 - e) % 4], r_y.at[e - 1, 4])
    b[4] = project(tokt[...].reshape(128, 1536), 1)
    to_diag = (y + 4 - x) % 4
    used_qt = used[0]
    used[0] += 1

    def text_query():
        return pltpu.make_async_remote_copy(
            src_ref=b.at[4, 0:96], dst_ref=qtraw.at[y], send_sem=send.at[used_qt],
            recv_sem=r_qt.at[to_diag - 1], device_id=at_seq(z, x, x), device_id_type=MESH,
        )

    @pl.when(diag)
    def _():
        qtraw[y] = b[4, 0:96]

    @pl.when(jnp.logical_not(diag))
    def _():
        text_query().start()

    for e in (2, 1, 3):
        copy_to(b.at[4, 96:288], kv.at[4, y], r_kv.at[e - 1, 4], ypeer(e))
    kv[4, y] = b[4, 96:288]

    set_keys(0)
    video_chunk(3)
    for d in (1, 3, 2):
        arrived(qraw.at[(y + d) % 4], r_q.at[(y + d) % 4])
    qall[x] = queries(by_rows(qraw), gq_v)
    for d in (1, 3, 2):
        copy_to(qall.at[x], qall.at[x], r_qx.at[d - 1, 0], xpeer(d))
    qt_first = used[0]
    used[0] += 3

    def text_queries(d):
        return pltpu.make_async_remote_copy(
            src_ref=qall.at[4], dst_ref=qall.at[4], send_sem=send.at[qt_first + d - 1],
            recv_sem=r_qx.at[0, 1], device_id=xpeer(d), device_id_type=MESH,
        )

    @pl.when(diag)
    def _():
        for d in (1, 3, 2):
            arrived(qtraw.at[(y + d) % 4], r_qt.at[d - 1])
        qall[4] = queries(by_rows(qtraw), gq_t)
        for d in (1, 3, 2):
            text_queries(d).start()

    for ch in (1, 2, 4, 3):
        set_keys(ch)
    @pl.when(y == z)
    def _():
        wo_own().wait()

    @pl.when(y != z)
    def _():
        arrived(wo.at[x, y], r_wo.at[y])

    for d in (1, 2, 3):
        arrived(wo.at[x, (y + d) % 4], r_wo.at[(y + d) % 4])

    for d in (1, 3, 2):
        copy_to(wo.at[x], wo.at[x], r_wox.at[d - 1], xpeer(d))

    for d in (1, 3, 2):
        arrived(qall.at[(x + 4 - d) % 4], r_qx.at[d - 1, 0])

    @pl.when(jnp.logical_not(diag))
    def _():
        arrived(qall.at[4], r_qx.at[0, 1])

    r = lax.broadcasted_iota(jnp.int32, (128, 256), 0)
    place = (r // 16) * (4 - 3 * odd) + x * (1 + 3 * odd)
    index = (((r % 16) // 4) * 16 + place) * 4 + r % 4
    usable = (r < 64) & (index < text_len[c])

    def attend(slots, h):
        wide = 128 * len(slots)
        queries_in = jnp.concatenate(
            [qall[slot, 128 * h : 128 * h + 128, :] for slot in slots], axis=1
        )
        scores = jnp.dot(kn[h], queries_in, preferred_element_type=F32) * FACTOR
        words = jnp.where(usable[:, 0:wide], scores[512:640], -1e30)
        scores = jnp.concatenate([scores[0:512], words], axis=0)
        highest = jnp.max(scores, axis=0, keepdims=True)
        weights = jnp.exp(scores - highest)
        total = jnp.sum(weights, axis=0, keepdims=True)
        out = jnp.dot(
            vall[128 * h : 128 * h + 128, :], weights.astype(BF16), preferred_element_type=F32
        )
        out = (out / total).astype(BF16)
        for i, slot in enumerate(slots):
            part = slice(128 * i, 128 * i + 128)
            osend[h, slot] = out[:, part]
            ssend[h, slot, 0:1, :] = highest[:, part]
            ssend[h, slot, 1:2, :] = total[:, part]

    ot_first = used[0]
    used[0] += 6
    at_first = used[0]
    used[0] += 9

    def text_out(h, i):
        a, bb = ((osend, otrecv), (ssend, strecv))[i]
        return pltpu.make_async_remote_copy(
            src_ref=a.at[h, 4], dst_ref=bb.at[h, x], send_sem=send.at[ot_first + 2 * h + i],
            recv_sem=r_ot.at[(x + 4 - y) % 4 - 1, h, i], device_id=at_seq(z, y, y),
            device_id_type=MESH,
        )

    def text_att(h, d):
        part = att.at[4, pl.ds(128 * h, 128)]
        return pltpu.make_async_remote_copy(
            src_ref=part, dst_ref=part, send_sem=send.at[at_first + 3 * h + d - 1],
            recv_sem=r_attt.at[h], device_id=ypeer(d), device_id_type=MESH,
        )

    def attend_head(h):
        def send_part(d):
            qc = (x + d) % 4
            copy_to(osend.at[h, qc], orecv.at[h, x], r_o.at[d - 1, h, 0], xpeer(d))
            copy_to(ssend.at[h, qc], srecv.at[h, x], r_o.at[d - 1, h, 1], xpeer(d))

        attend(((x + 2) % 4, (x + 1) % 4), h)
        send_part(2)
        send_part(1)
        attend(((x + 3) % 4, 4), h)
        send_part(3)

        @pl.when(diag)
        def _():
            otrecv[h, x] = osend[h, 4]
            strecv[h, x] = ssend[h, 4]

        @pl.when(jnp.logical_not(diag))
        def _():
            text_out(h, 0).start()
            text_out(h, 1).start()

        attend((x,), h)
        orecv[h, x] = osend[h, x]
        srecv[h, x] = ssend[h, x]

    def combine(o, st, h):
        top = [st[h, i, 0:1, :] for i in range(4)]
        highest = jnp.maximum(jnp.maximum(top[0], top[1]), jnp.maximum(top[2], top[3]))
        share = [st[h, i, 1:2, :] * jnp.exp(top[i] - highest) for i in range(4)]
        total = share[0] + share[1] + share[2] + share[3]
        acc = jnp.zeros((128, 128), F32)
        for i in range(4):
            acc += (share[i] / total) * o[h, i].astype(F32)
        return acc.astype(BF16)

    def combine_head(h):
        part = pl.ds(128 * h, 128)
        for d in (1, 3, 2):
            arrived(orecv.at[h, x], r_o.at[d - 1, h, 0])
            arrived(srecv.at[h, x], r_o.at[d - 1, h, 1])
        att[y, part] = combine(orecv, srecv, h)
        for d in (1, 3, 2):
            copy_to(att.at[y, part], att.at[y, part], r_att.at[d - 1, h], ypeer(d))

        @pl.when(diag)
        def _():
            for d in (1, 3, 2):
                arrived(otrecv.at[h, x], r_ot.at[d - 1, h, 0])
                arrived(strecv.at[h, x], r_ot.at[d - 1, h, 1])
            att[4, part] = combine(otrecv, strecv, h)
            for d in (1, 3, 2):
                text_att(h, d).start()

    attend_head(0)
    attend_head(1)
    combine_head(0)
    attend_head(2)
    combine_head(1)
    combine_head(2)
    for d in (1, 3, 2):
        arrived(wo.at[x], r_wox.at[d - 1])
    weights_out = wo[...].reshape(768, 384)

    def project_out(values, stream):
        out = jnp.dot(weights_out, values, preferred_element_type=F32)
        return natural(
            [
                out[(xx * 4 + yy) * 48 + stream * 24 :][:24]
                for yy in range(4)
                for xx in range(4)
            ]
        ).T

    def video_block(slot):
        block = project_out(att[slot], 0).astype(BF16)
        for q in range(4):
            for j in range(3):
                pout[slot, q, 32 * j : 32 * j + 32, :] = block[
                    32 * q : 32 * q + 32, 128 * j : 128 * j + 128
                ]

    video_block(y)

    own_first = used[0]
    used[0] += 8
    rows_of = (pl.ds(0, 96), pl.ds(96, 16))

    def own_row(dy, i):
        slot = (y + dy) % 4
        return pltpu.make_async_remote_copy(
            src_ref=pout.at[slot, y, rows_of[i]], dst_ref=precv.at[z, y, rows_of[i]],
            send_sem=send.at[own_first + 2 * dy + i], recv_sem=r_out.at[z, y, i],
            device_id=at_seq(slot, y, x), device_id_type=MESH,
        )

    def leave(dy, i):
        slot = (y + dy) % 4
        for e in (2, 1, 3):
            q = (y + e) % 4
            copy_to(
                pout.at[slot, q, rows_of[i]], precv.at[z, y, rows_of[i]], r_out.at[z, y, i],
                at_seq(slot, q, x),
            )

        @pl.when(slot == z)
        def _():
            precv[z, y, rows_of[i], :] = pout[slot, y, rows_of[i], :]

        @pl.when(slot != z)
        def _():
            own_row(dy, i).start()

    own_words[...] = unpack(zt[z].astype(F32))
    leave(0, 0)
    for dy in (1, 3, 2):
        slot = (y + dy) % 4
        for h in range(3):
            arrived(att.at[slot, pl.ds(128 * h, 128)], r_att.at[3 - dy, h])
        video_block(slot)
        leave(dy, 0)

    @pl.when(jnp.logical_not(diag))
    def _():
        for h in range(3):
            arrived(att.at[4, pl.ds(128 * h, 128)], r_attt.at[h])

    tall[...] = project_out(att[4], 1)
    for yy in range(4):
        for q in range(4):
            for j in range(3):
                pack32[4 * j : 4 * j + 4, 0:128] = tall[
                    16 * yy + 4 * q : 16 * yy + 4 * q + 4, 128 * j : 128 * j + 128
                ]
            pout[q, yy, 96:112, :] = pack32[:, 0:128].astype(BF16)

    for dy in (0, 1, 3, 2):
        leave(dy, 1)

    for dy in (0, 1, 3, 2):
        yy = (y + dy) % 4
        for dz in (0, 1, 3, 2):
            if dy or dz:
                for i in range(2):
                    arrived(precv.at[z, y, rows_of[i]], r_out.at[(z + dz) % 4, yy, i])
        total = precv[0, yy].astype(F32)
        for zz in range(1, 4):
            total += precv[zz, yy].astype(F32)
        total = total.astype(BF16).astype(F32)
        for j in range(3):
            at = pl.ds(pl.multiple_of(384 * yy + 128 * j, 128), 128)
            vout[:, at] = (
                zv[z, :, at].astype(F32) + mod[2:3, at] * total[32 * j : 32 * j + 32]
            ).astype(BF16)
            own = own_words[:, at]
            tout[:, at] = (own + mod[5:6, at] * total[96 + 4 * j : 100 + 4 * j]).astype(BF16)

    for op in always:
        op.wait_send()

    for k, d in enumerate(order):
        @pl.when((z + 4 - d) % 4 != y)
        def _():
            query_send(k, (z + 4 - d) % 4).wait_send()

        @pl.when((y + d) % 4 != z)
        def _():
            for i in range(2):
                own_row(d, i).wait_send()

    @pl.when(y != z)
    def _():
        wo_near().wait_send()

    @pl.when(diag)
    def _():
        for d in (1, 3, 2):
            text_queries(d).wait_send()
            for h in range(3):
                text_att(h, d).wait_send()

    @pl.when(jnp.logical_not(diag))
    def _():
        text_query().wait_send()
        for h in range(3):
            text_out(h, 0).wait_send()
            text_out(h, 1).wait_send()


def body(
    latent_video, text_embed, previous_video, previous_text, noise_blend, modulation,
    w_qkv, w_out, qk_gain, text_len, timestep,
):
    blend = noise_blend.T
    mod = modulation[0].transpose(0, 2, 1, 3)
    gains = qk_gain[0]
    wqkv = w_qkv[0].transpose(0, 1, 3, 2).reshape(144, 1536)
    wout = w_out[0].transpose(0, 2, 1).reshape(48, 1536)
    vm = pl.BlockSpec(memory_space=pltpu.VMEM)
    sm = pl.BlockSpec(memory_space=pltpu.SMEM)
    hbm = pl.BlockSpec(memory_space=pltpu.HBM)

    def buf(*shape, dtype=BF16):
        return pltpu.VMEM(shape, dtype)

    def sems(*shape):
        return pltpu.SemaphoreType.DMA(shape)

    video, words = pl.pallas_call(
        kernel,
        out_shape=(
            jax.ShapeDtypeStruct((32, 1536), BF16),
            jax.ShapeDtypeStruct((4, 1536), BF16),
        ),
        in_specs=[sm, sm] + [hbm] * 9,
        out_specs=(vm, vm),
        scratch_shapes=[
            buf(32, 1536), buf(4, 1536), buf(32, 1536), buf(4, 1536), buf(2, 50, dtype=F32),
            buf(50, 3, 2, 1536, dtype=F32), buf(2, 2, 128, dtype=F32), buf(8, 1536, dtype=F32),
            buf(4, 128, 128, dtype=F32),
            buf(32, 1536), buf(16, 384, dtype=F32), buf(16, 384),
            buf(4, 32, 1536), buf(4, 16, 384), buf(16, 32, 1536), buf(8, 16, 1536),
            buf(4, 144, 1536), buf(2, 288, 1536),
            buf(5, 288, 128), buf(5, 4, 192, 128), buf(4, 96, 128), buf(4, 96, 128),
            buf(5, 384, 128), buf(3, 640, 128), buf(384, 640),
            buf(3, 5, 128, 128), buf(3, 5, 8, 128, dtype=F32),
            buf(3, 4, 128, 128), buf(3, 4, 8, 128, dtype=F32),
            buf(3, 4, 128, 128), buf(3, 4, 8, 128, dtype=F32),
            buf(4, 4, 48, 384), buf(5, 384, 128), buf(128, 384, dtype=F32), buf(4, 1536, dtype=F32),
            buf(4, 4, 112, 128), buf(4, 4, 112, 128),
            sems(176), sems(4, 2), sems(3, 2), sems(3, 5), sems(4), sems(3), sems(3, 5),
            sems(3, 2), sems(3, 3, 2), sems(3, 3, 2), sems(4), sems(3), sems(3, 3), sems(3),
            sems(4, 4, 2), sems(9),
        ],
        compiler_params=pltpu.CompilerParams(
            collective_id=0, has_side_effects=True, vmem_limit_bytes=48 << 20
        ),
    )(
        timestep, text_len,
        *[
            pltpu.with_memory_space_constraint(a, pltpu.HBM)
            for a in (
                latent_video, text_embed, previous_video[0], previous_text[0],
                blend, mod, gains, wqkv, wout,
            )
        ],
    )
    return video[None], words[None]


def solution(mesh):
    placed = (
        P("seq", None),
        P("seq", None),
        P("comp", "seq", None),
        P("comp", "seq", None),
        P(),
        P("comp", None, None, None, None),
        P("comp", None, None, None, "seq"),
        P("comp", None, None, "seq"),
        P("comp", None, None, None),
        P(),
        P(),
    )
    return jax.shard_map(
        body,
        mesh=mesh,
        in_specs=placed,
        out_specs=(P("comp", "seq", None), P("comp", "seq", None)),
        check_vma=False,
    )
```
